1024 devices in a mesh: dp: 32 (over y, x_lo), seq: 32 (over z, x_hi, core).
Axes of the slice: x: 8 (x_hi: 2, x_lo: 4; x = x_hi * 4 + x_lo), y: 8, z: 8, core: 2. Of those that a mesh axis runs over, the one named last changes fastest.
Arguments:
- queries: bfloat16 [32, 4096, 512], P('dp', 'seq'), may hold values from -6 to 6
- keys: bfloat16 [32, 4096, 512], P('dp', 'seq'), may hold values from -6 to 6
- values: bfloat16 [32, 4096, 512], P('dp', 'seq'), may hold values from -6 to 6
- gates: bfloat16 [32, 4096, 512], P('dp', 'seq'), may hold values from -6 to 6
- lengths: int32 [32], P('dp'), may hold values from 1024 to 4096, as said below
- rab_steps: float32 [4, 16], replicated, may hold values from -3 to 3
- out_grad: bfloat16 [32, 4096, 512], P('dp', 'seq'), may hold values from -6 to 6
Outputs:
- gated: bfloat16 [32, 4096, 512], P('dp', 'seq')
- query_grad: bfloat16 [32, 4096, 512], P('dp', 'seq')
- key_grad: bfloat16 [32, 4096, 512], P('dp', 'seq')
- value_grad: bfloat16 [32, 4096, 512], P('dp', 'seq')
- gate_grad: bfloat16 [32, 4096, 512], P('dp', 'seq')
- rab_grad: float32 [4, 16], replicated
The draws below stay inside these ranges and needn't reach their ends.
Inputs may be any that keep to these rules, and one draw needn't show every extreme that they name: Events at and after position lengths[u] of user u are padding; some user fills all 4096 slots.
All inputs are finite; a program needn't handle non-finite values.
Results may differ from the reference program's by a relative error of at most 0.0057.
Values may be sent and summed in bfloat16 or wider, within the bound.
A program may use at most 64 MiB of HBM per device.

```python
import jax
import jax.numpy as jnp
from jax import lax

HEADS = 4
HEAD_DIM = 128
BUCKETS = 16
WIDTH = 512
LENGTH = 4096
USERS = 32


def draw_lengths(key, part):
    key = jax.random.fold_in(key, 7)
    first_key, second_key = jax.random.split(key)
    drawn = jax.random.randint(first_key, (USERS,), LENGTH // 4, LENGTH + 1)
    longest = jax.random.randint(second_key, (), 0, USERS)
    return jnp.where(jnp.arange(USERS) == longest, LENGTH, drawn).astype(jnp.int32)


def steps_of(own_key, dims, cuts, least, top_value):
    loudness, own = 1.0, jax.random.fold_in(own_key, 6)
    for dim, blocks in cuts:
        steps = jnp.exp(jax.random.uniform(jax.random.fold_in(own, dim), (blocks,), jnp.float32, least / len(cuts), top_value / len(cuts)))
        loudness = loudness * jnp.repeat(steps, dims[dim] // blocks).reshape([-1 if axis == dim else 1 for axis in range(len(dims))])
    return loudness


def noise(rng, shape, width, bound, shards=(), kind=jnp.bfloat16):
    factor_of = steps_of(rng, shape, shards, -0.22, 0.18) if shards else 1.0
    result = jax.random.normal(rng, shape, jnp.float32) * width * factor_of
    return jnp.minimum(jnp.maximum(result, -bound), bound).astype(kind)


def setup_inputs(seed: int = 0) -> dict:
    arg_keys = jax.random.split(jax.random.key(seed), 8)
    return {
        "queries": noise(arg_keys[0], (USERS, LENGTH, WIDTH), 1.0, 6.0, ((0, 32), (1, 32))),
        "keys": noise(arg_keys[1], (USERS, LENGTH, WIDTH), 1.0, 6.0, ((0, 32), (1, 32))),
        "values": noise(arg_keys[2], (USERS, LENGTH, WIDTH), 1.0, 6.0, ((0, 32), (1, 32))),
        "gates": noise(arg_keys[3], (USERS, LENGTH, WIDTH), 1.0, 6.0, ((0, 32), (1, 32))),
        "lengths": draw_lengths(jax.random.fold_in(arg_keys[7], 71), 0),
        "rab_steps": noise(arg_keys[5], (HEADS, BUCKETS), 0.5, 3.0, (), jnp.float32),
        "out_grad": noise(arg_keys[6], (USERS, LENGTH, WIDTH), 1.0, 6.0, ((0, 32), (1, 32))),
    }


def pair_terms(query_rows, key_rows, value_rows, dgrad_rows, query_pos, key_pos, rab_steps, valid_len):
    band_width = LENGTH // BUCKETS
    query_heads = query_rows.astype(jnp.float32).reshape(query_rows.shape[0], HEADS, HEAD_DIM)
    key_heads = key_rows.astype(jnp.float32).reshape(key_rows.shape[0], HEADS, HEAD_DIM)
    raw_score = jnp.einsum("ihd,jhd->hij", query_heads, key_heads) * (HEAD_DIM ** -0.5)
    offset = query_pos[:, None] - key_pos[None, :]
    live_mask = (offset >= 0) & (query_pos[:, None] < valid_len) & (key_pos[None, :] < valid_len)
    bias_sum = jnp.zeros(raw_score.shape, jnp.float32)
    for level in range(BUCKETS):
        ramp_mask = (offset >= level * band_width).astype(jnp.float32)
        bias_sum = bias_sum + rab_steps[:, level][:, None, None] * ramp_mask[None]
    pre_act = raw_score + bias_sum
    sigmoid_pre = jax.nn.sigmoid(pre_act)
    attn_scale = LENGTH ** -0.5
    weight = jnp.where(live_mask[None], pre_act * sigmoid_pre * attn_scale, 0.0)
    dgrad_heads = dgrad_rows.astype(jnp.float32).reshape(dgrad_rows.shape[0], HEADS, HEAD_DIM)
    value_heads = value_rows.astype(jnp.float32).reshape(value_rows.shape[0], HEADS, HEAD_DIM)
    dweight = jnp.einsum("ihd,jhd->hij", dgrad_heads, value_heads)
    dpre = jnp.where(live_mask[None], dweight * attn_scale * sigmoid_pre * (1.0 + pre_act * (1.0 - sigmoid_pre)), 0.0)
    return weight, dpre, offset


def band_sums(dpre, offset):
    band_width = LENGTH // BUCKETS
    columns = []
    for level in range(BUCKETS):
        ramp_mask = (offset >= level * band_width).astype(jnp.float32)
        columns.append(jnp.sum(dpre * ramp_mask[None], axis=(1, 2)))
    return jnp.stack(columns, axis=1)


def halved(array):
    return lax.optimization_barrier(array.astype(jnp.bfloat16)).astype(jnp.float32)


def reference(queries, keys, values, gates, lengths, rab_steps, out_grad):
    block_rows = min(512, LENGTH)
    inv_root = HEAD_DIM ** -0.5

    def one_user(packed):
        user_q, user_k, user_v, user_u, user_og, valid_len = packed
        dgrad = (user_og.astype(jnp.float32) * user_u.astype(jnp.float32)).astype(jnp.bfloat16)
        key_pos = jnp.arange(LENGTH, dtype=jnp.int32)
        key_heads = user_k.astype(jnp.float32).reshape(LENGTH, HEADS, HEAD_DIM)
        value_heads = user_v.astype(jnp.float32).reshape(LENGTH, HEADS, HEAD_DIM)

        def query_block(carry, index):
            key_acc, value_acc, rab_acc = carry
            start = (index * block_rows).astype(jnp.int32)
            query_rows = lax.dynamic_slice_in_dim(user_q, start, block_rows, 0)
            dgrad_rows = lax.dynamic_slice_in_dim(dgrad, start, block_rows, 0)
            query_pos = start + jnp.arange(block_rows, dtype=jnp.int32)
            weight, dpre, offset = pair_terms(query_rows, user_k, user_v, dgrad_rows, query_pos, key_pos, rab_steps, valid_len)
            weight_half = halved(weight)
            dpre_half = halved(dpre)
            query_heads = query_rows.astype(jnp.float32).reshape(block_rows, HEADS, HEAD_DIM)
            dgrad_heads = dgrad_rows.astype(jnp.float32).reshape(block_rows, HEADS, HEAD_DIM)
            attended = jnp.einsum("hij,jhd->ihd", weight_half, value_heads).reshape(block_rows, WIDTH)
            query_part = jnp.einsum("hij,jhd->ihd", dpre_half, key_heads).reshape(block_rows, WIDTH) * inv_root
            key_acc = key_acc + jnp.einsum("hij,ihd->jhd", dpre_half, query_heads).reshape(LENGTH, WIDTH) * inv_root
            value_acc = value_acc + jnp.einsum("hij,ihd->jhd", weight_half, dgrad_heads).reshape(LENGTH, WIDTH)
            rab_acc = rab_acc + band_sums(dpre, offset)
            return (key_acc, value_acc, rab_acc), (attended, query_part)

        start_carry = (jnp.zeros((LENGTH, WIDTH), jnp.float32), jnp.zeros((LENGTH, WIDTH), jnp.float32), jnp.zeros((HEADS, BUCKETS), jnp.float32))
        final_carry, stacked = lax.scan(query_block, start_carry, jnp.arange(LENGTH // block_rows, dtype=jnp.int32))
        key_acc, value_acc, rab_acc = final_carry
        attended = stacked[0].reshape(LENGTH, WIDTH)
        query_acc = stacked[1].reshape(LENGTH, WIDTH)
        gated = (attended * user_u.astype(jnp.float32)).astype(jnp.bfloat16)
        gate_grad = (user_og.astype(jnp.float32) * attended).astype(jnp.bfloat16)
        return gated, query_acc.astype(jnp.bfloat16), key_acc.astype(jnp.bfloat16), value_acc.astype(jnp.bfloat16), gate_grad, rab_acc

    results = lax.map(one_user, (queries, keys, values, gates, out_grad, lengths))
    rab_grad = jnp.sum(results[5], axis=0) / LENGTH
    return results[0], results[1], results[2], results[3], results[4], rab_grad
```

```python
import functools

import jax
import jax.numpy as jnp
from jax import lax
from jax.experimental import pallas as pl
from jax.experimental.pallas import tpu as pltpu
from jax.sharding import PartitionSpec as P

MESH = pl.DeviceIdType.MESH
BF16, F32 = jnp.bfloat16, jnp.float32
HEADS, DIM, BANDS = 4, 128, 16
ROWS, HALF = 128, 256
DEAD = -20000.0


def nt(a, b):
    return lax.dot_general(a, b, (((1,), (1,)), ((), ())), preferred_element_type=F32)


def nn(a, b):
    return jnp.dot(a, b, preferred_element_type=F32)


def tn(a, b):
    return lax.dot_general(a, b, (((0,), (0,)), ((), ())), preferred_element_type=F32)


def kernel(
    q_hbm, k_hbm, v_hbm, gate_hbm, og_hbm, len_ref, rab_ref,
    out_ref, rab_out,
    src, raw, obj, acc, snd, ret, stg, land, csm, low, tot,
    l_sem, a_s, a_r, f_s, f_r, b_s, b_r, o_s, o_r,
):
    sq = lax.axis_index("seq")
    z, xh, c = sq // 4, (sq // 2) % 2, sq % 2
    head = 2 * xh + c
    sign = 1 - 2 * c
    zp = c * 7 + sign * z
    prim, sec = 1 - c, c
    near, far = xh, 1 - xh

    def plane(rel):
        other_x = 1 - xh if rel & 2 else xh
        other_c = 1 - c if rel & 1 else c
        return other_x, other_c

    def at_plane(rel):
        other_x, other_c = plane(rel)
        return {"seq": z * 4 + other_x * 2 + other_c}

    def at_z(step):
        return {"seq": ((z + step * sign + 8) % 8) * 4 + xh * 2 + c}

    barrier = pltpu.get_barrier_semaphore()
    for rel in (1, 2, 3):
        pl.semaphore_signal(barrier, inc=1, device_id=at_plane(rel), device_id_type=MESH)
    for step in (1, -1, 2, -2, 3, -3):
        pl.semaphore_signal(barrier, inc=1, device_id=at_z(step), device_id_type=MESH)

    loads = [
        pltpu.make_async_copy(gate_hbm, raw.at[0], l_sem.at[0]),
        pltpu.make_async_copy(og_hbm, raw.at[1], l_sem.at[1]),
        pltpu.make_async_copy(q_hbm, src.at[0, 0], l_sem.at[2]),
        pltpu.make_async_copy(k_hbm, src.at[1, 0], l_sem.at[3]),
        pltpu.make_async_copy(v_hbm, src.at[1, 1], l_sem.at[4]),
    ]
    for load in loads:
        load.start()
    csm[0] = jnp.float32(DEAD)
    level = jnp.float32(0.0)
    for band in range(BANDS):
        level = level + rab_ref[head, band]
        csm[band + 1] = level * 0.5
    for load in loads[:2]:
        load.wait()
    row_at = sq * ROWS + lax.broadcasted_iota(jnp.int32, (ROWS, HEADS * DIM), 0)
    dgrad = raw[0].astype(F32) * raw[1].astype(F32)
    src[0, 1] = jnp.where(row_at < len_ref[0], dgrad, 0.0).astype(BF16)
    for load in loads[2:]:
        load.wait()
    pl.semaphore_wait(barrier, 9)

    def head_cols(which):
        return pl.ds(pl.multiple_of(which * DIM, DIM), DIM)

    def own_rows(which):
        return pl.ds(pl.multiple_of(which * ROWS, ROWS), ROWS)

    def exchange(rel, which):
        other_x, other_c = plane(rel)
        return pltpu.make_async_remote_copy(
            src_ref=src.at[which, :, :, head_cols(2 * other_x + other_c)],
            dst_ref=obj.at[which, xh, :, own_rows(c), :],
            send_sem=a_s.at[rel - 1, which],
            recv_sem=a_r.at[rel - 1, which],
            device_id=at_plane(rel),
            device_id_type=MESH,
        )

    def arrival(rel, which):
        other_x, other_c = plane(rel)
        return pltpu.make_async_remote_copy(
            src_ref=src.at[which, :, :, head_cols(head)],
            dst_ref=obj.at[which, other_x, :, own_rows(other_c), :],
            send_sem=a_s.at[rel - 1, which],
            recv_sem=a_r.at[rel - 1, which],
            device_id=at_plane(rel),
            device_id_type=MESH,
        )

    def leading(core):
        up = jnp.where(z >= 6, 0, 1)
        down = jnp.where(z < 2, 1, 0)
        return jnp.where(core == 0, up, down)

    mine, theirs = leading(c), leading(1 - c)
    exchange(2, mine).start()
    exchange(3, theirs).start()
    exchange(1, theirs).start()
    exchange(2, 1 - mine).start()
    exchange(3, 1 - theirs).start()
    exchange(1, 1 - theirs).start()
    for which in (0, 1):
        for part in (0, 1):
            obj[which, xh, part, own_rows(c), :] = src[which, part, :, head_cols(head)]

    def move(source, hop, dist, half, kind):
        return pltpu.make_async_remote_copy(
            src_ref=obj.at[source, half],
            dst_ref=obj.at[1 + dist, half],
            send_sem=f_s.at[kind, half],
            recv_sem=f_r.at[dist - 1, half],
            device_id=at_z(hop),
            device_id_type=MESH,
        )

    def own_slot(dist):
        return jnp.where(zp + dist < 8, prim, sec)

    def to_one(half):
        return move(own_slot(1), 1, 1, half, 0)

    def to_two(half):
        return move(own_slot(2), 2, 2, half, 1)

    def pass_three(half):
        return move(3, 1, 3, half, 2)

    def pass_four(half):
        return move(3, 2, 4, half, 3)

    def to_three(half):
        return move(sec, 3, 3, half, 4)

    gives_three = zp != 7
    gives_four = (zp >= 2) & (zp <= 5)
    has_four = zp >= 4

    def pass_on(half):
        to_two(half).wait_recv()

        @pl.when(gives_three)
        def _():
            pass_three(half).start()

        @pl.when(gives_four)
        def _():
            pass_four(half).start()

    arrival(1, mine).wait_recv()
    to_two(near).start()

    @pl.when(zp != 6)
    def _():
        to_one(near).start()

    arrival(2, mine).wait_recv()
    arrival(3, mine).wait_recv()
    to_two(far).start()

    @pl.when(zp != 6)
    def _():
        to_one(far).start()

    acc[...] = jnp.zeros_like(acc)
    low[...] = jnp.zeros_like(low)
    tot[...] = jnp.zeros_like(tot)
    pass_on(near)
    for rel in (1, 2, 3):
        arrival(rel, 1 - mine).wait_recv()

    @pl.when(zp == 6)
    def _():
        to_one(near).start()
        to_one(far).start()

    @pl.when(zp == 5)
    def _():
        to_three(near).start()
        to_three(far).start()

    pass_on(far)

    row = lax.broadcasted_iota(jnp.int32, (HALF, HALF), 0)
    col = lax.broadcasted_iota(jnp.int32, (HALF, HALF), 1)
    lower = row >= col

    def fold(tile):
        return jnp.sum(tile.reshape(HALF // 8, 8, HALF), axis=0)

    def pair(q_slot, q_half, k_slot, k_half, gap):
        query, dgr = obj[q_slot, q_half, 0], obj[q_slot, q_half, 1]
        key, value = obj[k_slot, k_half, 0], obj[k_slot, k_half, 1]
        half_act = nt(query, key) * (0.5 * DIM**-0.5) + jnp.where(lower, csm[gap + 1], csm[gap])
        th = jnp.tanh(half_act)
        up = 1.0 + th
        weight = (half_act * up).astype(BF16)
        dpre = nt(dgr, value) * (up * (1.0 + half_act * (1.0 - th)))
        dhalf = dpre.astype(BF16)
        acc[q_slot, q_half, 1] += nn(weight, value)
        acc[q_slot, q_half, 0] += nn(dhalf, key)
        acc[k_slot, k_half, 1] += tn(weight, dgr)
        acc[k_slot, k_half, 0] += tn(dhalf, query)
        tot[gap] += fold(dpre)
        low[gap] += fold(jnp.where(lower, dpre, 0.0))

    def diagonal(index, unused):
        q_half, k_half = jnp.minimum(index, 1), index // 2
        pair(0, q_half, 1, k_half, q_half - k_half)
        return unused

    lax.fori_loop(0, 3, diagonal, 0)

    def chunk(index, unused):
        dist = index // 2 + 1
        half = jnp.where(index % 2 == 0, near, far)

        @pl.when(dist != 2)
        def _():
            move(0, 1, dist, half, 0).wait_recv()

        slot = 1 + dist
        direct = zp >= dist
        kind = jnp.where(direct, prim, sec)
        gap = 2 * jnp.where(direct, dist, 8 - dist)
        q_slot = jnp.where(kind == 0, slot, 0)
        k_slot = jnp.where(kind == 0, 1, slot)
        for other in (0, 1):
            q_half = jnp.where(kind == 0, half, other)
            k_half = jnp.where(kind == 0, other, half)
            pair(q_slot, q_half, k_slot, k_half, gap + q_half - k_half)
        return unused

    lax.fori_loop(0, jnp.where(has_four, 8, 6), chunk, 0)

    def give_back(dist, hop, place, half):
        return pltpu.make_async_remote_copy(
            src_ref=snd.at[dist - 1, half],
            dst_ref=ret.at[place, half],
            send_sem=b_s.at[dist - 1, half],
            recv_sem=b_r.at[place, half],
            device_id=at_z(-hop),
            device_id_type=MESH,
        )

    def back_one(half):
        return give_back(1, 1, 2, half)

    def back_two(half):
        return give_back(2, 2, 3, half)

    def back_three(half):
        first = zp == 0
        return give_back(3, jnp.where(first, 3, 1), jnp.where(first, 4, 0), half)

    def back_four(half):
        return give_back(4, 2, 1, half)

    def ready(dist, half):
        snd[dist - 1, half] = acc[1 + dist, half].astype(BF16)

    def returned(place, half):
        give_back(1, 1, place, half).wait_recv()

    for half in (far, near):
        @pl.when(has_four)
        def _():
            ready(4, half)
            back_four(half).start()

        ready(3, half)
        back_three(half).start()
    for half in (far, near):
        ready(1, half)
        back_one(half).start()

    def deliver(rel, which):
        other_x, other_c = plane(rel)
        return pltpu.make_async_remote_copy(
            src_ref=stg.at[which, other_x, :, own_rows(other_c), :],
            dst_ref=land.at[which, :, :, head_cols(head)],
            send_sem=o_s.at[rel - 1, which],
            recv_sem=o_r.at[rel - 1, which],
            device_id=at_plane(rel),
            device_id_type=MESH,
        )

    def delivered(rel, which):
        other_x, other_c = plane(rel)
        return pltpu.make_async_remote_copy(
            src_ref=stg.at[which, other_x, :, own_rows(other_c), :],
            dst_ref=land.at[which, :, :, head_cols(2 * other_x + other_c)],
            send_sem=o_s.at[rel - 1, which],
            recv_sem=o_r.at[rel - 1, which],
            device_id=at_plane(rel),
            device_id_type=MESH,
        )

    def finish(which, half, is_far):
        stg[which, half, 0] = (acc[which, half, 0] * (DIM**-0.5 * 0.5 / 64.0)).astype(BF16)
        stg[which, half, 1] = (acc[which, half, 1] * (1.0 / 64.0)).astype(BF16)
        if is_far:
            deliver(2, which).start()
            deliver(3, which).start()
        else:
            deliver(1, which).start()
            for part in (0, 1):
                land[which, part, :, head_cols(head)] = stg[which, half, part, own_rows(c), :]

    late = own_slot(2)
    both_late = (zp == 5) | (zp == 6)

    @pl.when(jnp.logical_not(both_late))
    def _():
        finish(1 - late, far, True)
        finish(1 - late, near, False)

    for half in (far, near):
        @pl.when(gives_three)
        def _():
            returned(0, half)
            acc[3, half] += ret[0, half].astype(F32)

        @pl.when(gives_four)
        def _():
            returned(1, half)
            acc[3, half] += ret[1, half].astype(F32)

        ready(2, half)
        back_two(half).start()
    for half, is_far in ((far, True), (near, False)):
        returned(2, half)
        acc[own_slot(1), half] += ret[2, half].astype(F32)
        returned(3, half)
        acc[late, half] += ret[3, half].astype(F32)

        @pl.when(zp == 5)
        def _():
            returned(4, half)
            acc[sec, half] += ret[4, half].astype(F32)

        finish(late, half, is_far)

        @pl.when(both_late)
        def _():
            finish(1 - late, half, is_far)

    rows_out = [None] * BANDS
    running = jnp.zeros((1, HALF), F32)
    for band in range(BANDS - 1, -1, -1):
        rows_out[band] = running + jnp.sum(low[band], axis=0, keepdims=True)
        running = running + jnp.sum(tot[band], axis=0, keepdims=True)
    per_band = jnp.sum(jnp.concatenate(rows_out, axis=0), axis=1, keepdims=True)
    lane = lax.broadcasted_iota(jnp.int32, (BANDS, DIM), 1)
    line = lax.broadcasted_iota(jnp.int32, (BANDS, DIM), 0)
    spread = jnp.sum(jnp.where(lane == line, per_band, 0.0), axis=0, keepdims=True)
    place = lax.broadcasted_iota(jnp.int32, (8, DIM), 0)
    rab_out[...] = jnp.where(place == head, spread * (0.5 / 64.0 / 4096.0), 0.0)

    for which in (0, 1):
        for rel in (1, 2, 3):
            delivered(rel, which).wait_recv()
    out_ref[...] = land[...]

    for which in (0, 1):
        for rel in (1, 2, 3):
            exchange(rel, which).wait_send()
            deliver(rel, which).wait_send()
    for half in (far, near):
        to_one(half).wait_send()
        to_two(half).wait_send()
        back_one(half).wait_send()
        back_two(half).wait_send()
        back_three(half).wait_send()

        @pl.when(gives_three)
        def _():
            pass_three(half).wait_send()

        @pl.when(gives_four)
        def _():
            pass_four(half).wait_send()

        @pl.when(zp == 5)
        def _():
            to_three(half).wait_send()

        @pl.when(has_four)
        def _():
            back_four(half).wait_send()


def body(queries, keys, values, gates, lengths, rab_steps, out_grad):
    block = (2, 2, HALF, DIM)
    any_space = pl.BlockSpec(memory_space=pl.ANY)
    smem = pl.BlockSpec(memory_space=pltpu.SMEM)
    vmem = pl.BlockSpec(memory_space=pltpu.VMEM)
    dma = pltpu.SemaphoreType.DMA
    landed, rab_part = pl.pallas_call(
        kernel,
        out_shape=(
            jax.ShapeDtypeStruct((2, 2, ROWS, HEADS * DIM), BF16),
            jax.ShapeDtypeStruct((8, DIM), F32),
        ),
        in_specs=[any_space] * 5 + [smem] * 2,
        out_specs=(vmem, vmem),
        scratch_shapes=[
            pltpu.VMEM((2, 2, ROWS, HEADS * DIM), BF16),
            pltpu.VMEM((2, ROWS, HEADS * DIM), BF16),
            pltpu.VMEM((6,) + block, BF16),
            pltpu.VMEM((6,) + block, F32),
            pltpu.VMEM((4,) + block, BF16),
            pltpu.VMEM((5,) + block, BF16),
            pltpu.VMEM((2,) + block, BF16),
            pltpu.VMEM((2, 2, ROWS, HEADS * DIM), BF16),
            pltpu.SMEM((BANDS + 1,), F32),
            pltpu.VMEM((BANDS, 8, HALF), F32),
            pltpu.VMEM((BANDS, 8, HALF), F32),
            dma((5,)),
            dma((3, 2)),
            dma((3, 2)),
            dma((5, 2)),
            dma((4, 2)),
            dma((4, 2)),
            dma((5, 2)),
            dma((3, 2)),
            dma((3, 2)),
        ],
        compiler_params=pltpu.CompilerParams(
            collective_id=0, has_side_effects=True, vmem_limit_bytes=40 * 2**20
        ),
        name="attend",
    )(queries[0], keys[0], values[0], gates[0], out_grad[0], lengths, rab_steps)
    rab_grad = lax.psum(rab_part[:HEADS, :BANDS], ("dp", "seq"))
    row_at = lax.axis_index("seq") * ROWS + jnp.arange(ROWS, dtype=jnp.int32)[:, None]
    attended = jnp.where(row_at < lengths[0], landed[0, 1].astype(F32), 0.0)
    gated = (attended * gates[0].astype(F32)).astype(BF16)
    gate_grad = (attended * out_grad[0].astype(F32)).astype(BF16)
    return gated[None], landed[0, 0][None], landed[1, 0][None], landed[1, 1][None], gate_grad[None], rab_grad


def solution(mesh):
    rows = P("dp", "seq", None)
    return jax.shard_map(
        body,
        mesh=mesh,
        in_specs=(rows, rows, rows, rows, P("dp"), P(), rows),
        out_specs=(rows, rows, rows, rows, rows, P()),
        check_vma=False,
    )
```

```python
import functools

import jax
import jax.numpy as jnp
from jax import lax
from jax.experimental import pallas as pl
from jax.experimental.pallas import tpu as pltpu
from jax.sharding import PartitionSpec as P

MESH = pl.DeviceIdType.MESH
BF16, F32 = jnp.bfloat16, jnp.float32
HEADS, DIM, BANDS = 4, 128, 16
ROWS, HALF = 128, 256
DEAD = -20000.0


def nt(a, b):
    return lax.dot_general(a, b, (((1,), (1,)), ((), ())), preferred_element_type=F32)


def nn(a, b):
    return jnp.dot(a, b, preferred_element_type=F32)


def tn(a, b):
    return lax.dot_general(a, b, (((0,), (0,)), ((), ())), preferred_element_type=F32)


def kernel(
    q_hbm, k_hbm, v_hbm, gate_hbm, og_hbm, len_ref, rab_ref,
    out_ref, rab_out,
    src, raw, obj, acc, snd, ret, stg, land, csm, low, tot,
    msg, got,
    l_sem, a_s, a_r, f_s, f_r, b_s, b_r, o_s, o_r, r_s, r_r,
):
    dp, sq = lax.axis_index("dp"), lax.axis_index("seq")
    y, xl = dp // 4, dp % 4
    z, xh, c = sq // 4, (sq // 2) % 2, sq % 2
    head = 2 * xh + c
    sign = 1 - 2 * c
    zp = c * 7 + sign * z
    prim, sec = 1 - c, c
    near, far = xh, 1 - xh

    def plane(rel):
        other_x = 1 - xh if rel & 2 else xh
        other_c = 1 - c if rel & 1 else c
        return other_x, other_c

    def at_plane(rel):
        other_x, other_c = plane(rel)
        return {"seq": z * 4 + other_x * 2 + other_c}

    def at_z(step):
        return {"seq": ((z + step * sign + 8) % 8) * 4 + xh * 2 + c}

    barrier = pltpu.get_barrier_semaphore()
    for rel in (1, 2, 3):
        pl.semaphore_signal(barrier, inc=1, device_id=at_plane(rel), device_id_type=MESH)
    for step in range(1, 8):
        pl.semaphore_signal(barrier, inc=1, device_id=at_z(step), device_id_type=MESH)
        pl.semaphore_signal(barrier, inc=1, device_id={"dp": ((y + step) % 8) * 4 + xl}, device_id_type=MESH)
    for step in range(1, 4):
        pl.semaphore_signal(barrier, inc=1, device_id={"dp": y * 4 + (xl + step) % 4}, device_id_type=MESH)

    loads = [
        pltpu.make_async_copy(gate_hbm, raw.at[0], l_sem.at[0]),
        pltpu.make_async_copy(og_hbm, raw.at[1], l_sem.at[1]),
        pltpu.make_async_copy(q_hbm, src.at[0, 0], l_sem.at[2]),
        pltpu.make_async_copy(k_hbm, src.at[1, 0], l_sem.at[3]),
        pltpu.make_async_copy(v_hbm, src.at[1, 1], l_sem.at[4]),
    ]
    for load in loads:
        load.start()
    csm[0] = jnp.float32(DEAD)
    level = jnp.float32(0.0)
    for band in range(BANDS):
        level = level + rab_ref[head, band]
        csm[band + 1] = level * 0.5
    for load in loads[:2]:
        load.wait()
    row_at = sq * ROWS + lax.broadcasted_iota(jnp.int32, (ROWS, HEADS * DIM), 0)
    dgrad = raw[0].astype(F32) * raw[1].astype(F32)
    src[0, 1] = jnp.where(row_at < len_ref[0], dgrad, 0.0).astype(BF16)
    for load in loads[2:]:
        load.wait()
    pl.semaphore_wait(barrier, 20)

    def head_cols(which):
        return pl.ds(pl.multiple_of(which * DIM, DIM), DIM)

    def own_rows(which):
        return pl.ds(pl.multiple_of(which * ROWS, ROWS), ROWS)

    def exchange(rel, which):
        other_x, other_c = plane(rel)
        return pltpu.make_async_remote_copy(
            src_ref=src.at[which, :, :, head_cols(2 * other_x + other_c)],
            dst_ref=obj.at[which, xh, :, own_rows(c), :],
            send_sem=a_s.at[rel - 1, which],
            recv_sem=a_r.at[rel - 1, which],
            device_id=at_plane(rel),
            device_id_type=MESH,
        )

    def arrival(rel, which):
        other_x, other_c = plane(rel)
        return pltpu.make_async_remote_copy(
            src_ref=src.at[which, :, :, head_cols(head)],
            dst_ref=obj.at[which, other_x, :, own_rows(other_c), :],
            send_sem=a_s.at[rel - 1, which],
            recv_sem=a_r.at[rel - 1, which],
            device_id=at_plane(rel),
            device_id_type=MESH,
        )

    def leading(core):
        up = jnp.where(z >= 6, 0, 1)
        down = jnp.where(z < 2, 1, 0)
        return jnp.where(core == 0, up, down)

    mine, theirs = leading(c), leading(1 - c)
    exchange(2, mine).start()
    exchange(3, theirs).start()
    exchange(1, theirs).start()
    exchange(2, 1 - mine).start()
    exchange(3, 1 - theirs).start()
    exchange(1, 1 - theirs).start()
    for which in (0, 1):
        for part in (0, 1):
            obj[which, xh, part, own_rows(c), :] = src[which, part, :, head_cols(head)]

    def move(source, hop, dist, half, part, kind):
        return pltpu.make_async_remote_copy(
            src_ref=obj.at[source, half, part],
            dst_ref=obj.at[1 + dist, half, part],
            send_sem=f_s.at[kind, half, part],
            recv_sem=f_r.at[dist - 1, half, part],
            device_id=at_z(hop),
            device_id_type=MESH,
        )

    late = jnp.where(zp < 7, prim, sec)
    jump = jnp.where(zp == 6, 2, 3)

    def to_next(half, part):
        return move(late, 1, 1, half, part, 0)

    def along(dist, half, part):
        return move(1 + dist, 1, dist + 1, half, part, dist)

    def across(half, part):
        return move(sec, jump, jump, half, part, 4)

    def hands_on(dist):
        return (zp >= 1) & (zp <= 4) if dist == 3 else zp != 7

    has_four = (zp >= 2) & (zp <= 5)
    jumps = (zp == 5) | (zp == 6)

    def start_both(copy_of, half):
        for part in (0, 1):
            copy_of(half, part).start()

    def pass_on(dist, half):
        for part in (0, 1):
            move(0, 1, dist, half, part, 0).wait_recv()

            @pl.when(hands_on(dist))
            def _():
                along(dist, half, part).start()

    def leave(half):
        @pl.when(zp != 6)
        def _():
            start_both(to_next, half)

        @pl.when(zp == 6)
        def _():
            start_both(across, half)

    arrival(1, mine).wait_recv()
    leave(near)
    acc[...] = jnp.zeros_like(acc)
    low[...] = jnp.zeros_like(low)
    tot[...] = jnp.zeros_like(tot)
    pass_on(1, near)
    arrival(2, mine).wait_recv()
    arrival(3, mine).wait_recv()
    leave(far)
    pass_on(2, near)
    pass_on(3, near)
    pass_on(1, far)
    for rel in (1, 2, 3):
        arrival(rel, 1 - mine).wait_recv()
    for half in (near, far):
        @pl.when(zp == 6)
        def _():
            start_both(to_next, half)

        @pl.when(zp == 5)
        def _():
            start_both(across, half)

    row = lax.broadcasted_iota(jnp.int32, (HALF, HALF), 0)
    col = lax.broadcasted_iota(jnp.int32, (HALF, HALF), 1)
    lower = row >= col

    def fold(tile):
        return jnp.sum(tile.reshape(HALF // 8, 8, HALF), axis=0)

    def pair(q_slot, q_half, k_slot, k_half, gap):
        query, dgr = obj[q_slot, q_half, 0], obj[q_slot, q_half, 1]
        key, value = obj[k_slot, k_half, 0], obj[k_slot, k_half, 1]
        half_act = nt(query, key) * (0.5 * DIM**-0.5) + jnp.where(lower, csm[gap + 1], csm[gap])
        th = jnp.tanh(half_act)
        up = 1.0 + th
        weight = (half_act * up).astype(BF16)
        dpre = nt(dgr, value) * (up * (1.0 + half_act * (1.0 - th)))
        dhalf = dpre.astype(BF16)
        acc[q_slot, q_half, 1] += nn(weight, value)
        acc[q_slot, q_half, 0] += nn(dhalf, key)
        acc[k_slot, k_half, 1] += tn(weight, dgr)
        acc[k_slot, k_half, 0] += tn(dhalf, query)
        tot[gap] += fold(dpre)
        low[gap] += fold(jnp.where(lower, dpre, 0.0))

    def diagonal(index, unused):
        q_half, k_half = jnp.minimum(index, 1), index // 2
        pair(0, q_half, 1, k_half, q_half - k_half)
        return unused

    lax.fori_loop(0, 3, diagonal, 0)

    def chunk(index, unused):
        dist = jnp.where(index >= 6, 4, index % 3 + 1)
        half = jnp.where((index < 3) | (index == 6), near, far)

        @pl.when(index == 1)
        def _():
            pass_on(2, far)

        @pl.when(index == 4)
        def _():
            pass_on(3, far)

        @pl.when(index >= 6)
        def _():
            for part in (0, 1):
                move(0, 1, 4, half, part, 0).wait_recv()

        slot = 1 + dist
        direct = zp >= dist
        kind = jnp.where(direct, prim, sec)
        gap = 2 * jnp.where(direct, dist, 8 - dist)
        q_slot = jnp.where(kind == 0, slot, 0)
        k_slot = jnp.where(kind == 0, 1, slot)
        for other in (0, 1):
            q_half = jnp.where(kind == 0, half, other)
            k_half = jnp.where(kind == 0, other, half)
            pair(q_slot, q_half, k_slot, k_half, gap + q_half - k_half)
        return unused

    lax.fori_loop(0, jnp.where(has_four, 8, 6), chunk, 0)

    def give_back(dist, half, part):
        jumped = (zp == 0) if dist in (2, 3) else False
        place = jnp.where(jumped, 4, dist - 1)
        return pltpu.make_async_remote_copy(
            src_ref=snd.at[dist - 1, half, part],
            dst_ref=ret.at[place, half, part],
            send_sem=b_s.at[dist - 1, half, part],
            recv_sem=b_r.at[place, half, part],
            device_id=at_z(jnp.where(jumped, -dist, -1)),
            device_id_type=MESH,
        )

    def take_back(slot, place, half, part):
        pltpu.make_async_remote_copy(
            src_ref=snd.at[0, half, part],
            dst_ref=ret.at[place, half, part],
            send_sem=b_s.at[0, half, part],
            recv_sem=b_r.at[place, half, part],
            device_id=at_z(-1),
            device_id_type=MESH,
        ).wait_recv()
        acc[slot, half, part] += ret[place, half, part].astype(F32)

    def send_back(dist):
        for half in (far, near):
            for part in (0, 1):
                if dist < 4:
                    @pl.when(hands_on(dist))
                    def _():
                        take_back(1 + dist, dist, half, part)

                snd[dist - 1, half, part] = acc[1 + dist, half, part].astype(BF16)
                give_back(dist, half, part).start()

    rows_out = [None] * BANDS
    running = jnp.zeros((1, HALF), F32)
    for band in range(BANDS - 1, -1, -1):
        rows_out[band] = running + jnp.sum(low[band], axis=0, keepdims=True)
        running = running + jnp.sum(tot[band], axis=0, keepdims=True)
    per_band = jnp.sum(jnp.concatenate(rows_out, axis=0), axis=1, keepdims=True)
    lane = lax.broadcasted_iota(jnp.int32, (BANDS, DIM), 1)
    line = lax.broadcasted_iota(jnp.int32, (BANDS, DIM), 0)
    spread = jnp.sum(jnp.where(lane == line, per_band, 0.0), axis=0, keepdims=True)
    place = lax.broadcasted_iota(jnp.int32, (8, DIM), 0)
    share = jnp.where(place == head, spread * (0.5 / 64.0 / 4096.0), 0.0)

    def stage(phase):
        if phase == 0:
            return 8, z, lambda other: {"seq": other * 4 + head}
        if phase == 1:
            return 8, y, lambda other: {"dp": other * 4 + xl}
        if phase == 2:
            return 4, xl, lambda other: {"dp": y * 4 + other}
        return 4, head, lambda other: {"seq": z * 4 + other}

    def share_with(phase, step):
        count, here, place_of = stage(phase)
        other = (here + step) % count
        return pltpu.make_async_remote_copy(
            src_ref=msg.at[phase],
            dst_ref=got.at[phase, here],
            send_sem=r_s.at[phase, step],
            recv_sem=r_r.at[phase, here],
            device_id=place_of(other),
            device_id_type=MESH,
        )

    def shared_by(phase, step):
        count, here, place_of = stage(phase)
        other = (here + step) % count
        return pltpu.make_async_remote_copy(
            src_ref=msg.at[phase],
            dst_ref=got.at[phase, other],
            send_sem=r_s.at[phase, step],
            recv_sem=r_r.at[phase, other],
            device_id=place_of(other),
            device_id_type=MESH,
        )

    def send_share(phase, value):
        count, here, _ = stage(phase)
        msg[phase] = value
        for step in range(1, count):
            share_with(phase, step).start()
        got[phase, here] = value

    def sum_shares(phase):
        count, _, _ = stage(phase)
        for step in range(1, count):
            shared_by(phase, step).wait_recv()
        total = got[phase, 0]
        for other in range(1, count):
            total = total + got[phase, other]
        return total

    send_share(0, share)

    @pl.when(has_four)
    def _():
        send_back(4)

    def deliver(rel, which):
        other_x, other_c = plane(rel)
        return pltpu.make_async_remote_copy(
            src_ref=stg.at[which, other_x, :, own_rows(other_c), :],
            dst_ref=land.at[which, :, :, head_cols(head)],
            send_sem=o_s.at[rel - 1, which],
            recv_sem=o_r.at[rel - 1, which],
            device_id=at_plane(rel),
            device_id_type=MESH,
        )

    def delivered(rel, which):
        other_x, other_c = plane(rel)
        return pltpu.make_async_remote_copy(
            src_ref=stg.at[which, other_x, :, own_rows(other_c), :],
            dst_ref=land.at[which, :, :, head_cols(2 * other_x + other_c)],
            send_sem=o_s.at[rel - 1, which],
            recv_sem=o_r.at[rel - 1, which],
            device_id=at_plane(rel),
            device_id_type=MESH,
        )

    def finish(which, half, is_far):
        stg[which, half, 0] = (acc[which, half, 0] * (DIM**-0.5 * 0.5 / 64.0)).astype(BF16)
        stg[which, half, 1] = (acc[which, half, 1] * (1.0 / 64.0)).astype(BF16)
        if is_far:
            deliver(2, which).start()
            deliver(3, which).start()
        else:
            deliver(1, which).start()
            for part in (0, 1):
                land[which, part, :, head_cols(head)] = stg[which, half, part, own_rows(c), :]

    @pl.when(jnp.logical_not(jumps))
    def _():
        finish(1 - late, far, True)
        finish(1 - late, near, False)

    send_back(3)
    send_share(1, sum_shares(0))
    send_back(2)
    send_back(1)
    for half, is_far in ((far, True), (near, False)):
        for part in (0, 1):
            take_back(late, 0, half, part)

        @pl.when(jumps)
        def _():
            for part in (0, 1):
                take_back(sec, 4, half, part)

        finish(late, half, is_far)

        @pl.when(jumps)
        def _():
            finish(1 - late, half, is_far)

        send_share(2 if is_far else 3, sum_shares(1 if is_far else 2))

    for which in (0, 1):
        for rel in (1, 2, 3):
            delivered(rel, which).wait_recv()
    rab_out[...] = sum_shares(3)
    out_ref[...] = land[...]
    for phase in range(4):
        for step in range(1, stage(phase)[0]):
            share_with(phase, step).wait_send()

    for which in (0, 1):
        for rel in (1, 2, 3):
            exchange(rel, which).wait_send()
            deliver(rel, which).wait_send()
    for half in (far, near):
        for part in (0, 1):
            to_next(half, part).wait_send()
            for dist in (1, 2, 3):
                give_back(dist, half, part).wait_send()

                @pl.when(hands_on(dist))
                def _():
                    along(dist, half, part).wait_send()

            @pl.when(jumps)
            def _():
                across(half, part).wait_send()

            @pl.when(has_four)
            def _():
                give_back(4, half, part).wait_send()


def body(queries, keys, values, gates, lengths, rab_steps, out_grad):
    block = (2, 2, HALF, DIM)
    any_space = pl.BlockSpec(memory_space=pl.ANY)
    smem = pl.BlockSpec(memory_space=pltpu.SMEM)
    vmem = pl.BlockSpec(memory_space=pltpu.VMEM)
    dma = pltpu.SemaphoreType.DMA
    landed, rab_part = pl.pallas_call(
        kernel,
        out_shape=(
            jax.ShapeDtypeStruct((2, 2, ROWS, HEADS * DIM), BF16),
            jax.ShapeDtypeStruct((8, DIM), F32),
        ),
        in_specs=[any_space] * 5 + [smem] * 2,
        out_specs=(vmem, vmem),
        scratch_shapes=[
            pltpu.VMEM((2, 2, ROWS, HEADS * DIM), BF16),
            pltpu.VMEM((2, ROWS, HEADS * DIM), BF16),
            pltpu.VMEM((6,) + block, BF16),
            pltpu.VMEM((6,) + block, F32),
            pltpu.VMEM((4,) + block, BF16),
            pltpu.VMEM((5,) + block, BF16),
            pltpu.VMEM((2,) + block, BF16),
            pltpu.VMEM((2, 2, ROWS, HEADS * DIM), BF16),
            pltpu.SMEM((BANDS + 1,), F32),
            pltpu.VMEM((BANDS, 8, HALF), F32),
            pltpu.VMEM((BANDS, 8, HALF), F32),
            pltpu.VMEM((4, 8, DIM), F32),
            pltpu.VMEM((4, 8, 8, DIM), F32),
            dma((5,)),
            dma((3, 2)),
            dma((3, 2)),
            dma((5, 2, 2)),
            dma((4, 2, 2)),
            dma((4, 2, 2)),
            dma((5, 2, 2)),
            dma((3, 2)),
            dma((3, 2)),
            dma((4, 8)),
            dma((4, 8)),
        ],
        compiler_params=pltpu.CompilerParams(
            collective_id=0, has_side_effects=True, vmem_limit_bytes=60 * 2**20
        ),
        name="attend",
    )(queries[0], keys[0], values[0], gates[0], out_grad[0], lengths, rab_steps)
    rab_grad = rab_part[:HEADS, :BANDS]
    row_at = lax.axis_index("seq") * ROWS + jnp.arange(ROWS, dtype=jnp.int32)[:, None]
    attended = jnp.where(row_at < lengths[0], landed[0, 1].astype(F32), 0.0)
    gated = (attended * gates[0].astype(F32)).astype(BF16)
    gate_grad = (attended * out_grad[0].astype(F32)).astype(BF16)
    return gated[None], landed[0, 0][None], landed[1, 0][None], landed[1, 1][None], gate_grad[None], rab_grad


def solution(mesh):
    rows = P("dp", "seq", None)
    return jax.shard_map(
        body,
        mesh=mesh,
        in_specs=(rows, rows, rows, rows, P("dp"), P(), rows),
        out_specs=(rows, rows, rows, rows, rows, P()),
        check_vma=False,
    )
```

```python
import functools

import jax
import jax.numpy as jnp
from jax import lax
from jax.experimental import pallas as pl
from jax.experimental.pallas import tpu as pltpu
from jax.sharding import PartitionSpec as P

MESH = pl.DeviceIdType.MESH
BF16, F32 = jnp.bfloat16, jnp.float32
HEADS, DIM, BANDS = 4, 128, 16
ROWS, HALF = 128, 256
DEAD = -20000.0


def nt(a, b):
    return lax.dot_general(a, b, (((1,), (1,)), ((), ())), preferred_element_type=F32)


def nn(a, b):
    return jnp.dot(a, b, preferred_element_type=F32)


def tn(a, b):
    return lax.dot_general(a, b, (((0,), (0,)), ((), ())), preferred_element_type=F32)


def kernel(
    q_hbm, k_hbm, v_hbm, gate_hbm, og_hbm, len_ref, rab_ref,
    out_ref, rab_out,
    src, raw, obj, acc, snd, ret, stg, land, csm, low, tot,
    msg, got,
    l_sem, a_s, a_r, f_s, f_r, b_s, b_r, o_s, o_r, r_s, r_r,
):
    dp, sq = lax.axis_index("dp"), lax.axis_index("seq")
    y, xl = dp // 4, dp % 4
    z, xh, c = sq // 4, (sq // 2) % 2, sq % 2
    head = 2 * xh + c
    sign = 1 - 2 * c
    zp = c * 7 + sign * z
    prim, sec = 1 - c, c
    near, far = xh, 1 - xh

    def plane(rel):
        other_x = 1 - xh if rel & 2 else xh
        other_c = 1 - c if rel & 1 else c
        return other_x, other_c

    def at_plane(rel):
        other_x, other_c = plane(rel)
        return {"seq": z * 4 + other_x * 2 + other_c}

    def at_z(step):
        return {"seq": ((z + step * sign + 8) % 8) * 4 + xh * 2 + c}

    barrier = pltpu.get_barrier_semaphore()
    for rel in (1, 2, 3):
        pl.semaphore_signal(barrier, inc=1, device_id=at_plane(rel), device_id_type=MESH)
    for step in range(1, 8):
        pl.semaphore_signal(barrier, inc=1, device_id=at_z(step), device_id_type=MESH)
        pl.semaphore_signal(barrier, inc=1, device_id={"dp": ((y + step) % 8) * 4 + xl}, device_id_type=MESH)
    for step in range(1, 4):
        pl.semaphore_signal(barrier, inc=1, device_id={"dp": y * 4 + (xl + step) % 4}, device_id_type=MESH)

    loads = [
        pltpu.make_async_copy(gate_hbm, raw.at[0], l_sem.at[0]),
        pltpu.make_async_copy(og_hbm, raw.at[1], l_sem.at[1]),
        pltpu.make_async_copy(q_hbm, src.at[0, 0], l_sem.at[2]),
        pltpu.make_async_copy(k_hbm, src.at[1, 0], l_sem.at[3]),
        pltpu.make_async_copy(v_hbm, src.at[1, 1], l_sem.at[4]),
    ]
    for load in loads:
        load.start()
    csm[0] = jnp.float32(DEAD)
    level = jnp.float32(0.0)
    for band in range(BANDS):
        level = level + rab_ref[head, band]
        csm[band + 1] = level * 0.5
    for load in loads[:2]:
        load.wait()
    row_at = sq * ROWS + lax.broadcasted_iota(jnp.int32, (ROWS, HEADS * DIM), 0)
    dgrad = raw[0].astype(F32) * raw[1].astype(F32)
    src[0, 1] = jnp.where(row_at < len_ref[0], dgrad, 0.0).astype(BF16)
    for load in loads[2:]:
        load.wait()
    pl.semaphore_wait(barrier, 20)

    def head_cols(which):
        return pl.ds(pl.multiple_of(which * DIM, DIM), DIM)

    def own_rows(which):
        return pl.ds(pl.multiple_of(which * ROWS, ROWS), ROWS)

    def exchange(rel, which):
        other_x, other_c = plane(rel)
        return pltpu.make_async_remote_copy(
            src_ref=src.at[which, :, :, head_cols(2 * other_x + other_c)],
            dst_ref=obj.at[which, xh, :, own_rows(c), :],
            send_sem=a_s.at[rel - 1, which],
            recv_sem=a_r.at[rel - 1, which],
            device_id=at_plane(rel),
            device_id_type=MESH,
        )

    def arrival(rel, which):
        other_x, other_c = plane(rel)
        return pltpu.make_async_remote_copy(
            src_ref=src.at[which, :, :, head_cols(head)],
            dst_ref=obj.at[which, other_x, :, own_rows(other_c), :],
            send_sem=a_s.at[rel - 1, which],
            recv_sem=a_r.at[rel - 1, which],
            device_id=at_plane(rel),
            device_id_type=MESH,
        )

    def leading(core):
        up = jnp.where(z >= 6, 0, 1)
        down = jnp.where(z < 2, 1, 0)
        return jnp.where(core == 0, up, down)

    mine, theirs = leading(c), leading(1 - c)
    exchange(2, mine).start()
    exchange(3, theirs).start()
    exchange(1, theirs).start()
    exchange(2, 1 - mine).start()
    exchange(3, 1 - theirs).start()
    exchange(1, 1 - theirs).start()
    for which in (0, 1):
        for part in (0, 1):
            obj[which, xh, part, own_rows(c), :] = src[which, part, :, head_cols(head)]

    def move(source, hop, dist, half, kind):
        return pltpu.make_async_remote_copy(
            src_ref=obj.at[source, half],
            dst_ref=obj.at[1 + dist, half],
            send_sem=f_s.at[kind, half],
            recv_sem=f_r.at[dist - 1, half],
            device_id=at_z(hop),
            device_id_type=MESH,
        )

    late = jnp.where(zp < 7, prim, sec)

    def to_one(half):
        return move(late, 1, 1, half, 0)

    def to_two(half):
        return move(jnp.where(zp < 6, prim, sec), 2, 2, half, 1)

    def pass_three(half):
        return move(3, 1, 3, half, 2)

    def pass_four(half):
        return move(3, 2, 4, half, 3)

    def to_three(half):
        return move(sec, 3, 3, half, 4)

    gives_three = zp != 7
    gives_four = zp <= 3
    has_four = (zp >= 2) & (zp <= 5)
    jumps = (zp == 5) | (zp == 6)

    def sums_up(dist):
        return (zp >= 1) & (zp <= 4) if dist == 3 else zp != 7

    def pass_on(half):
        move(0, 2, 2, half, 1).wait_recv()

        @pl.when(gives_three)
        def _():
            pass_three(half).start()

        @pl.when(gives_four)
        def _():
            pass_four(half).start()

    def leave(half):
        to_two(half).start()

        @pl.when(zp != 6)
        def _():
            to_one(half).start()

    arrival(1, mine).wait_recv()
    leave(near)
    acc[...] = jnp.zeros_like(acc)
    low[...] = jnp.zeros_like(low)
    tot[...] = jnp.zeros_like(tot)
    arrival(2, mine).wait_recv()
    arrival(3, mine).wait_recv()
    leave(far)
    pass_on(near)
    for rel in (1, 2, 3):
        arrival(rel, 1 - mine).wait_recv()

    @pl.when(zp == 6)
    def _():
        to_one(near).start()
        to_one(far).start()

    @pl.when(zp == 5)
    def _():
        to_three(near).start()
        to_three(far).start()

    pass_on(far)

    row = lax.broadcasted_iota(jnp.int32, (HALF, HALF), 0)
    col = lax.broadcasted_iota(jnp.int32, (HALF, HALF), 1)
    lower = row >= col

    def fold(tile):
        return jnp.sum(tile.reshape(HALF // 8, 8, HALF), axis=0)

    def pair(q_slot, q_half, k_slot, k_half, gap):
        query, dgr = obj[q_slot, q_half, 0], obj[q_slot, q_half, 1]
        key, value = obj[k_slot, k_half, 0], obj[k_slot, k_half, 1]
        half_act = nt(query, key) * (0.5 * DIM**-0.5) + jnp.where(lower, csm[gap + 1], csm[gap])
        th = jnp.tanh(half_act)
        up = 1.0 + th
        weight = (half_act * up).astype(BF16)
        dpre = nt(dgr, value) * (up * (1.0 + half_act * (1.0 - th)))
        dhalf = dpre.astype(BF16)
        acc[q_slot, q_half, 1] += nn(weight, value)
        acc[q_slot, q_half, 0] += nn(dhalf, key)
        acc[k_slot, k_half, 1] += tn(weight, dgr)
        acc[k_slot, k_half, 0] += tn(dhalf, query)
        tot[gap] += fold(dpre)
        low[gap] += fold(jnp.where(lower, dpre, 0.0))

    def diagonal(index, unused):
        q_half, k_half = jnp.minimum(index, 1), index // 2
        pair(0, q_half, 1, k_half, q_half - k_half)
        return unused

    lax.fori_loop(0, 3, diagonal, 0)

    def chunk(index, unused):
        dist = index // 2 + 1
        half = jnp.where(index % 2 == 0, near, far)

        @pl.when(dist != 2)
        def _():
            move(0, 1, dist, half, 0).wait_recv()

        slot = 1 + dist
        direct = zp >= dist
        kind = jnp.where(direct, prim, sec)
        gap = 2 * jnp.where(direct, dist, 8 - dist)
        q_slot = jnp.where(kind == 0, slot, 0)
        k_slot = jnp.where(kind == 0, 1, slot)
        for other in (0, 1):
            q_half = jnp.where(kind == 0, half, other)
            k_half = jnp.where(kind == 0, other, half)
            pair(q_slot, q_half, k_slot, k_half, gap + q_half - k_half)
        return unused

    lax.fori_loop(0, jnp.where(has_four, 8, 6), chunk, 0)

    def give_back(dist, half, part):
        jumped = (zp == 0) if dist in (2, 3) else False
        place = jnp.where(jumped, 4, dist - 1)
        return pltpu.make_async_remote_copy(
            src_ref=snd.at[dist - 1, half, part],
            dst_ref=ret.at[place, half, part],
            send_sem=b_s.at[dist - 1, half, part],
            recv_sem=b_r.at[place, half, part],
            device_id=at_z(jnp.where(jumped, -dist, -1)),
            device_id_type=MESH,
        )

    def take_back(slot, place, half, part):
        pltpu.make_async_remote_copy(
            src_ref=snd.at[0, half, part],
            dst_ref=ret.at[place, half, part],
            send_sem=b_s.at[0, half, part],
            recv_sem=b_r.at[place, half, part],
            device_id=at_z(-1),
            device_id_type=MESH,
        ).wait_recv()
        acc[slot, half, part] += ret[place, half, part].astype(F32)

    def send_back(dist):
        for half in (far, near):
            for part in (0, 1):
                if dist < 4:
                    @pl.when(sums_up(dist))
                    def _():
                        take_back(1 + dist, dist, half, part)

                snd[dist - 1, half, part] = acc[1 + dist, half, part].astype(BF16)
                give_back(dist, half, part).start()

    rows_out = [None] * BANDS
    running = jnp.zeros((1, HALF), F32)
    for band in range(BANDS - 1, -1, -1):
        rows_out[band] = running + jnp.sum(low[band], axis=0, keepdims=True)
        running = running + jnp.sum(tot[band], axis=0, keepdims=True)
    per_band = jnp.sum(jnp.concatenate(rows_out, axis=0), axis=1, keepdims=True)
    lane = lax.broadcasted_iota(jnp.int32, (BANDS, DIM), 1)
    line = lax.broadcasted_iota(jnp.int32, (BANDS, DIM), 0)
    spread = jnp.sum(jnp.where(lane == line, per_band, 0.0), axis=0, keepdims=True)
    place = lax.broadcasted_iota(jnp.int32, (8, DIM), 0)
    share = jnp.where(place == head, spread * (0.5 / 64.0 / 4096.0), 0.0)

    def stage(phase):
        if phase == 0:
            return 8, z, lambda other: {"seq": other * 4 + head}
        if phase == 1:
            return 4, head, lambda other: {"seq": z * 4 + other}
        if phase == 2:
            return 4, xl, lambda other: {"dp": y * 4 + other}
        return 8, y, lambda other: {"dp": other * 4 + xl}

    def share_with(phase, step):
        count, here, place_of = stage(phase)
        other = (here + step) % count
        return pltpu.make_async_remote_copy(
            src_ref=msg.at[phase],
            dst_ref=got.at[phase, here],
            send_sem=r_s.at[phase, step],
            recv_sem=r_r.at[phase, here],
            device_id=place_of(other),
            device_id_type=MESH,
        )

    def shared_by(phase, step):
        count, here, place_of = stage(phase)
        other = (here + step) % count
        return pltpu.make_async_remote_copy(
            src_ref=msg.at[phase],
            dst_ref=got.at[phase, other],
            send_sem=r_s.at[phase, step],
            recv_sem=r_r.at[phase, other],
            device_id=place_of(other),
            device_id_type=MESH,
        )

    def send_share(phase, value):
        count, here, _ = stage(phase)
        msg[phase] = value
        for step in range(1, count):
            share_with(phase, step).start()
        got[phase, here] = value

    def sum_shares(phase):
        count, _, _ = stage(phase)
        for step in range(1, count):
            shared_by(phase, step).wait_recv()
        total = got[phase, 0]
        for other in range(1, count):
            total = total + got[phase, other]
        return total

    send_share(0, share)

    @pl.when(has_four)
    def _():
        send_back(4)

    def deliver(rel, which):
        other_x, other_c = plane(rel)
        return pltpu.make_async_remote_copy(
            src_ref=stg.at[which, other_x, :, own_rows(other_c), :],
            dst_ref=land.at[which, :, :, head_cols(head)],
            send_sem=o_s.at[rel - 1, which],
            recv_sem=o_r.at[rel - 1, which],
            device_id=at_plane(rel),
            device_id_type=MESH,
        )

    def delivered(rel, which):
        other_x, other_c = plane(rel)
        return pltpu.make_async_remote_copy(
            src_ref=stg.at[which, other_x, :, own_rows(other_c), :],
            dst_ref=land.at[which, :, :, head_cols(2 * other_x + other_c)],
            send_sem=o_s.at[rel - 1, which],
            recv_sem=o_r.at[rel - 1, which],
            device_id=at_plane(rel),
            device_id_type=MESH,
        )

    def finish(which, half, is_far):
        stg[which, half, 0] = (acc[which, half, 0] * (DIM**-0.5 * 0.5 / 64.0)).astype(BF16)
        stg[which, half, 1] = (acc[which, half, 1] * (1.0 / 64.0)).astype(BF16)
        if is_far:
            deliver(2, which).start()
            deliver(3, which).start()
        else:
            deliver(1, which).start()
            for part in (0, 1):
                land[which, part, :, head_cols(head)] = stg[which, half, part, own_rows(c), :]

    @pl.when(jnp.logical_not(jumps))
    def _():
        finish(1 - late, far, True)
        finish(1 - late, near, False)

    send_back(3)
    send_share(1, sum_shares(0))
    send_back(2)
    send_back(1)
    send_share(2, sum_shares(1))
    for half, is_far in ((far, True), (near, False)):
        for part in (0, 1):
            take_back(late, 0, half, part)

        @pl.when(jumps)
        def _():
            for part in (0, 1):
                take_back(sec, 4, half, part)

        finish(late, half, is_far)

        @pl.when(jumps)
        def _():
            finish(1 - late, half, is_far)

    send_share(3, sum_shares(2))
    for which in (0, 1):
        for rel in (1, 2, 3):
            delivered(rel, which).wait_recv()
    rab_out[...] = sum_shares(3)
    out_ref[...] = land[...]
    for phase in range(4):
        for step in range(1, stage(phase)[0]):
            share_with(phase, step).wait_send()

    for which in (0, 1):
        for rel in (1, 2, 3):
            exchange(rel, which).wait_send()
            deliver(rel, which).wait_send()
    for half in (far, near):
        to_one(half).wait_send()
        to_two(half).wait_send()

        @pl.when(gives_three)
        def _():
            pass_three(half).wait_send()

        @pl.when(gives_four)
        def _():
            pass_four(half).wait_send()

        @pl.when(zp == 5)
        def _():
            to_three(half).wait_send()

        for part in (0, 1):
            for dist in (1, 2, 3):
                give_back(dist, half, part).wait_send()

            @pl.when(has_four)
            def _():
                give_back(4, half, part).wait_send()


def body(queries, keys, values, gates, lengths, rab_steps, out_grad):
    block = (2, 2, HALF, DIM)
    any_space = pl.BlockSpec(memory_space=pl.ANY)
    smem = pl.BlockSpec(memory_space=pltpu.SMEM)
    vmem = pl.BlockSpec(memory_space=pltpu.VMEM)
    dma = pltpu.SemaphoreType.DMA
    landed, rab_part = pl.pallas_call(
        kernel,
        out_shape=(
            jax.ShapeDtypeStruct((2, 2, ROWS, HEADS * DIM), BF16),
            jax.ShapeDtypeStruct((8, DIM), F32),
        ),
        in_specs=[any_space] * 5 + [smem] * 2,
        out_specs=(vmem, vmem),
        scratch_shapes=[
            pltpu.VMEM((2, 2, ROWS, HEADS * DIM), BF16),
            pltpu.VMEM((2, ROWS, HEADS * DIM), BF16),
            pltpu.VMEM((6,) + block, BF16),
            pltpu.VMEM((6,) + block, F32),
            pltpu.VMEM((4,) + block, BF16),
            pltpu.VMEM((5,) + block, BF16),
            pltpu.VMEM((2,) + block, BF16),
            pltpu.VMEM((2, 2, ROWS, HEADS * DIM), BF16),
            pltpu.SMEM((BANDS + 1,), F32),
            pltpu.VMEM((BANDS, 8, HALF), F32),
            pltpu.VMEM((BANDS, 8, HALF), F32),
            pltpu.VMEM((4, 8, DIM), F32),
            pltpu.VMEM((4, 8, 8, DIM), F32),
            dma((5,)),
            dma((3, 2)),
            dma((3, 2)),
            dma((5, 2)),
            dma((4, 2)),
            dma((4, 2, 2)),
            dma((5, 2, 2)),
            dma((3, 2)),
            dma((3, 2)),
            dma((4, 8)),
            dma((4, 8)),
        ],
        compiler_params=pltpu.CompilerParams(
            collective_id=0, has_side_effects=True, vmem_limit_bytes=60 * 2**20
        ),
        name="attend",
    )(queries[0], keys[0], values[0], gates[0], out_grad[0], lengths, rab_steps)
    rab_grad = rab_part[:HEADS, :BANDS]
    row_at = lax.axis_index("seq") * ROWS + jnp.arange(ROWS, dtype=jnp.int32)[:, None]
    attended = jnp.where(row_at < lengths[0], landed[0, 1].astype(F32), 0.0)
    gated = (attended * gates[0].astype(F32)).astype(BF16)
    gate_grad = (attended * out_grad[0].astype(F32)).astype(BF16)
    return gated[None], landed[0, 0][None], landed[1, 0][None], landed[1, 1][None], gate_grad[None], rab_grad


def solution(mesh):
    rows = P("dp", "seq", None)
    return jax.shard_map(
        body,
        mesh=mesh,
        in_specs=(rows, rows, rows, rows, P("dp"), P(), rows),
        out_specs=(rows, rows, rows, rows, rows, P()),
        check_vma=False,
    )
```

```python
import functools

import jax
import jax.numpy as jnp
from jax import lax
from jax.experimental import pallas as pl
from jax.experimental.pallas import tpu as pltpu
from jax.sharding import PartitionSpec as P

MESH = pl.DeviceIdType.MESH
BF16, F32 = jnp.bfloat16, jnp.float32
HEADS, DIM, BANDS = 4, 128, 16
ROWS, HALF = 128, 256
DEAD = -20000.0


def nt(a, b):
    return lax.dot_general(a, b, (((1,), (1,)), ((), ())), preferred_element_type=F32)


def nn(a, b):
    return jnp.dot(a, b, preferred_element_type=F32)


def tn(a, b):
    return lax.dot_general(a, b, (((0,), (0,)), ((), ())), preferred_element_type=F32)


def kernel(
    q_hbm, k_hbm, v_hbm, gate_hbm, og_hbm, len_ref, rab_ref,
    out_ref, rab_out,
    src, raw, obj, acc, snd, ret, stg, land, csm, low, tot,
    msg, got,
    l_sem, a_s, a_r, f_s, f_r, b_s, b_r, o_s, o_r, r_s, r_r,
):
    dp, sq = lax.axis_index("dp"), lax.axis_index("seq")
    y, xl = dp // 4, dp % 4
    z, xh, c = sq // 4, (sq // 2) % 2, sq % 2
    head = 2 * xh + c
    sign = 1 - 2 * c
    zp = c * 7 + sign * z
    prim, sec = 1 - c, c
    near, far = xh, 1 - xh

    def plane(rel):
        other_x = 1 - xh if rel & 2 else xh
        other_c = 1 - c if rel & 1 else c
        return other_x, other_c

    def at_plane(rel):
        other_x, other_c = plane(rel)
        return {"seq": z * 4 + other_x * 2 + other_c}

    def at_z(step):
        return {"seq": ((z + step * sign + 8) % 8) * 4 + xh * 2 + c}

    barrier = pltpu.get_barrier_semaphore()
    for rel in (1, 2, 3):
        pl.semaphore_signal(barrier, inc=1, device_id=at_plane(rel), device_id_type=MESH)
    for step in range(1, 8):
        pl.semaphore_signal(barrier, inc=1, device_id=at_z(step), device_id_type=MESH)
        pl.semaphore_signal(barrier, inc=1, device_id={"dp": ((y + step) % 8) * 4 + xl}, device_id_type=MESH)
    for step in range(1, 4):
        pl.semaphore_signal(barrier, inc=1, device_id={"dp": y * 4 + (xl + step) % 4}, device_id_type=MESH)

    loads = [
        pltpu.make_async_copy(gate_hbm, raw.at[0], l_sem.at[0]),
        pltpu.make_async_copy(og_hbm, raw.at[1], l_sem.at[1]),
        pltpu.make_async_copy(q_hbm, src.at[0, 0], l_sem.at[2]),
        pltpu.make_async_copy(k_hbm, src.at[1, 0], l_sem.at[3]),
        pltpu.make_async_copy(v_hbm, src.at[1, 1], l_sem.at[4]),
    ]
    for load in loads:
        load.start()
    csm[0] = jnp.float32(DEAD)
    level = jnp.float32(0.0)
    for band in range(BANDS):
        level = level + rab_ref[head, band]
        csm[band + 1] = level * 0.5
    for load in loads[:2]:
        load.wait()
    row_at = sq * ROWS + lax.broadcasted_iota(jnp.int32, (ROWS, HEADS * DIM), 0)
    dgrad = raw[0].astype(F32) * raw[1].astype(F32)
    src[0, 1] = jnp.where(row_at < len_ref[0], dgrad, 0.0).astype(BF16)
    for load in loads[2:]:
        load.wait()
    pl.semaphore_wait(barrier, 20)

    def head_cols(which):
        return pl.ds(pl.multiple_of(which * DIM, DIM), DIM)

    def own_rows(which):
        return pl.ds(pl.multiple_of(which * ROWS, ROWS), ROWS)

    def exchange(rel, which):
        other_x, other_c = plane(rel)
        return pltpu.make_async_remote_copy(
            src_ref=src.at[which, :, :, head_cols(2 * other_x + other_c)],
            dst_ref=obj.at[which, xh, :, own_rows(c), :],
            send_sem=a_s.at[rel - 1, which],
            recv_sem=a_r.at[rel - 1, which],
            device_id=at_plane(rel),
            device_id_type=MESH,
        )

    def arrival(rel, which):
        other_x, other_c = plane(rel)
        return pltpu.make_async_remote_copy(
            src_ref=src.at[which, :, :, head_cols(head)],
            dst_ref=obj.at[which, other_x, :, own_rows(other_c), :],
            send_sem=a_s.at[rel - 1, which],
            recv_sem=a_r.at[rel - 1, which],
            device_id=at_plane(rel),
            device_id_type=MESH,
        )

    def leading(core):
        up = jnp.where(z >= 6, 0, 1)
        down = jnp.where(z < 2, 1, 0)
        return jnp.where(core == 0, up, down)

    mine, theirs = leading(c), leading(1 - c)
    exchange(2, mine).start()
    exchange(3, theirs).start()
    exchange(1, theirs).start()
    exchange(2, 1 - mine).start()
    exchange(3, 1 - theirs).start()
    exchange(1, 1 - theirs).start()
    for which in (0, 1):
        for part in (0, 1):
            obj[which, xh, part, own_rows(c), :] = src[which, part, :, head_cols(head)]

    def move(source, hop, dist, half, kind):
        return pltpu.make_async_remote_copy(
            src_ref=obj.at[source, half],
            dst_ref=obj.at[1 + dist, half],
            send_sem=f_s.at[kind, half],
            recv_sem=f_r.at[dist - 1, half],
            device_id=at_z(hop),
            device_id_type=MESH,
        )

    late = jnp.where(zp < 7, prim, sec)

    def to_one(half):
        return move(late, 1, 1, half, 0)

    def to_two(half):
        return move(jnp.where(zp < 6, prim, sec), 2, 2, half, 1)

    def pass_three(half):
        return move(3, 1, 3, half, 2)

    def pass_four(half):
        return move(3, 2, 4, half, 3)

    def to_three(half):
        return move(sec, 3, 3, half, 4)

    gives_three = zp != 7
    gives_four = zp <= 3
    has_four = (zp >= 2) & (zp <= 5)
    jumps = (zp == 5) | (zp == 6)

    def sums_up(dist):
        return (zp >= 1) & (zp <= 4) if dist == 3 else zp != 7

    def pass_on(half):
        move(0, 2, 2, half, 1).wait_recv()

        @pl.when(gives_three)
        def _():
            pass_three(half).start()

        @pl.when(gives_four)
        def _():
            pass_four(half).start()

    def leave(half):
        to_two(half).start()

        @pl.when(zp != 6)
        def _():
            to_one(half).start()

    arrival(1, mine).wait_recv()
    leave(near)
    acc[...] = jnp.zeros_like(acc)
    low[...] = jnp.zeros_like(low)
    tot[...] = jnp.zeros_like(tot)
    arrival(2, mine).wait_recv()
    arrival(3, mine).wait_recv()
    leave(far)
    pass_on(near)
    for rel in (1, 2, 3):
        arrival(rel, 1 - mine).wait_recv()

    @pl.when(zp == 6)
    def _():
        to_one(near).start()
        to_one(far).start()

    @pl.when(zp == 5)
    def _():
        to_three(near).start()
        to_three(far).start()

    pass_on(far)

    row = lax.broadcasted_iota(jnp.int32, (HALF, HALF), 0)
    col = lax.broadcasted_iota(jnp.int32, (HALF, HALF), 1)
    lower = row >= col

    def fold(tile):
        return jnp.sum(tile.reshape(HALF // 8, 8, HALF), axis=0)

    def pair(q_slot, q_half, k_slot, k_half, gap):
        query, dgr = obj[q_slot, q_half, 0], obj[q_slot, q_half, 1]
        key, value = obj[k_slot, k_half, 0], obj[k_slot, k_half, 1]
        half_act = nt(query, key) * (0.5 * DIM**-0.5) + jnp.where(lower, csm[gap + 1], csm[gap])
        th = jnp.tanh(half_act)
        up = 1.0 + th
        weight = (half_act * up).astype(BF16)
        dpre = nt(dgr, value) * (up * (1.0 + half_act * (1.0 - th)))
        dhalf = dpre.astype(BF16)
        acc[q_slot, q_half, 1] += nn(weight, value)
        acc[q_slot, q_half, 0] += nn(dhalf, key)
        acc[k_slot, k_half, 1] += tn(weight, dgr)
        acc[k_slot, k_half, 0] += tn(dhalf, query)
        tot[gap] += fold(dpre)
        low[gap] += fold(jnp.where(lower, dpre, 0.0))

    def diagonal(index, unused):
        q_half, k_half = jnp.minimum(index, 1), index // 2
        pair(0, q_half, 1, k_half, q_half - k_half)
        return unused

    lax.fori_loop(0, 3, diagonal, 0)

    def chunk(index, unused):
        dist = index // 2 + 1
        half = jnp.where(index % 2 == 0, near, far)

        @pl.when(dist != 2)
        def _():
            move(0, 1, dist, half, 0).wait_recv()

        slot = 1 + dist
        direct = zp >= dist
        kind = jnp.where(direct, prim, sec)
        gap = 2 * jnp.where(direct, dist, 8 - dist)
        q_slot = jnp.where(kind == 0, slot, 0)
        k_slot = jnp.where(kind == 0, 1, slot)
        for other in (0, 1):
            q_half = jnp.where(kind == 0, half, other)
            k_half = jnp.where(kind == 0, other, half)
            pair(q_slot, q_half, k_slot, k_half, gap + q_half - k_half)
        return unused

    lax.fori_loop(0, jnp.where(has_four, 8, 6), chunk, 0)

    def give_back(dist, half):
        jumped = (zp == 0) if dist == 3 else False
        hop = 2 if dist == 2 else jnp.where(jumped, 3, 1)
        place = jnp.where(jumped, 4, dist - 1)
        return pltpu.make_async_remote_copy(
            src_ref=snd.at[dist - 1, half],
            dst_ref=ret.at[place, half],
            send_sem=b_s.at[dist - 1, half],
            recv_sem=b_r.at[place, half],
            device_id=at_z(-hop),
            device_id_type=MESH,
        )

    def take_back(slot, place, half):
        pltpu.make_async_remote_copy(
            src_ref=snd.at[0, half],
            dst_ref=ret.at[place, half],
            send_sem=b_s.at[0, half],
            recv_sem=b_r.at[place, half],
            device_id=at_z(-1),
            device_id_type=MESH,
        ).wait_recv()
        acc[slot, half] += ret[place, half].astype(F32)

    def send_back(dist, half):
        if dist in (2, 3):
            @pl.when(sums_up(dist))
            def _():
                take_back(1 + dist, dist, half)

        snd[dist - 1, half] = acc[1 + dist, half].astype(BF16)
        give_back(dist, half).start()

    rows_out = [None] * BANDS
    running = jnp.zeros((1, HALF), F32)
    for band in range(BANDS - 1, -1, -1):
        rows_out[band] = running + jnp.sum(low[band], axis=0, keepdims=True)
        running = running + jnp.sum(tot[band], axis=0, keepdims=True)
    per_band = jnp.sum(jnp.concatenate(rows_out, axis=0), axis=1, keepdims=True)
    lane = lax.broadcasted_iota(jnp.int32, (BANDS, DIM), 1)
    line = lax.broadcasted_iota(jnp.int32, (BANDS, DIM), 0)
    spread = jnp.sum(jnp.where(lane == line, per_band, 0.0), axis=0, keepdims=True)
    place = lax.broadcasted_iota(jnp.int32, (8, DIM), 0)
    share = jnp.where(place == head, spread * (0.5 / 64.0 / 4096.0), 0.0)

    def stage(phase):
        if phase == 0:
            return 8, z, lambda other: {"seq": other * 4 + head}
        if phase == 1:
            return 4, head, lambda other: {"seq": z * 4 + other}
        if phase == 2:
            return 4, xl, lambda other: {"dp": y * 4 + other}
        return 8, y, lambda other: {"dp": other * 4 + xl}

    def share_with(phase, step):
        count, here, place_of = stage(phase)
        other = (here + step) % count
        return pltpu.make_async_remote_copy(
            src_ref=msg.at[phase],
            dst_ref=got.at[phase, here],
            send_sem=r_s.at[phase, step],
            recv_sem=r_r.at[phase, here],
            device_id=place_of(other),
            device_id_type=MESH,
        )

    def shared_by(phase, step):
        count, here, place_of = stage(phase)
        other = (here + step) % count
        return pltpu.make_async_remote_copy(
            src_ref=msg.at[phase],
            dst_ref=got.at[phase, other],
            send_sem=r_s.at[phase, step],
            recv_sem=r_r.at[phase, other],
            device_id=place_of(other),
            device_id_type=MESH,
        )

    def send_share(phase, value):
        count, here, _ = stage(phase)
        msg[phase] = value
        for step in range(1, count):
            share_with(phase, step).start()
        got[phase, here] = value

    def sum_shares(phase):
        count, _, _ = stage(phase)
        for step in range(1, count):
            shared_by(phase, step).wait_recv()
        total = got[phase, 0]
        for other in range(1, count):
            total = total + got[phase, other]
        return total

    send_share(0, share)

    for half in (far, near):
        @pl.when(has_four)
        def _():
            send_back(4, half)

        send_back(1, half)

    def deliver(rel, which):
        other_x, other_c = plane(rel)
        return pltpu.make_async_remote_copy(
            src_ref=stg.at[which, other_x, :, own_rows(other_c), :],
            dst_ref=land.at[which, :, :, head_cols(head)],
            send_sem=o_s.at[rel - 1, which],
            recv_sem=o_r.at[rel - 1, which],
            device_id=at_plane(rel),
            device_id_type=MESH,
        )

    def delivered(rel, which):
        other_x, other_c = plane(rel)
        return pltpu.make_async_remote_copy(
            src_ref=stg.at[which, other_x, :, own_rows(other_c), :],
            dst_ref=land.at[which, :, :, head_cols(2 * other_x + other_c)],
            send_sem=o_s.at[rel - 1, which],
            recv_sem=o_r.at[rel - 1, which],
            device_id=at_plane(rel),
            device_id_type=MESH,
        )

    def finish(which, half, is_far):
        stg[which, half, 0] = (acc[which, half, 0] * (DIM**-0.5 * 0.5 / 64.0)).astype(BF16)
        stg[which, half, 1] = (acc[which, half, 1] * (1.0 / 64.0)).astype(BF16)
        if is_far:
            deliver(2, which).start()
            deliver(3, which).start()
        else:
            deliver(1, which).start()
            for part in (0, 1):
                land[which, part, :, head_cols(head)] = stg[which, half, part, own_rows(c), :]

    @pl.when(jnp.logical_not(jumps))
    def _():
        finish(1 - late, far, True)
        finish(1 - late, near, False)

    send_back(3, far)
    send_back(3, near)
    send_share(1, sum_shares(0))
    send_back(2, far)
    send_back(2, near)
    send_share(2, sum_shares(1))
    for half, is_far in ((far, True), (near, False)):
        take_back(late, 0, half)
        take_back(jnp.where(zp < 6, prim, sec), 1, half)

        @pl.when(zp == 5)
        def _():
            take_back(sec, 4, half)

        finish(late, half, is_far)

        @pl.when(jumps)
        def _():
            finish(1 - late, half, is_far)

    send_share(3, sum_shares(2))
    for which in (0, 1):
        for rel in (1, 2, 3):
            delivered(rel, which).wait_recv()
    rab_out[...] = sum_shares(3)
    out_ref[...] = land[...]
    for phase in range(4):
        for step in range(1, stage(phase)[0]):
            share_with(phase, step).wait_send()

    for which in (0, 1):
        for rel in (1, 2, 3):
            exchange(rel, which).wait_send()
            deliver(rel, which).wait_send()
    for half in (far, near):
        to_one(half).wait_send()
        to_two(half).wait_send()

        @pl.when(gives_three)
        def _():
            pass_three(half).wait_send()

        @pl.when(gives_four)
        def _():
            pass_four(half).wait_send()

        @pl.when(zp == 5)
        def _():
            to_three(half).wait_send()

        for dist in (1, 2, 3):
            give_back(dist, half).wait_send()

        @pl.when(has_four)
        def _():
            give_back(4, half).wait_send()


def closing(landed, rab_in, gate, outgrad, len_ref, gated, q_grad, k_grad, v_grad, gate_grad, rab_grad):
    row_at = lax.axis_index("seq") * ROWS + lax.broadcasted_iota(jnp.int32, (ROWS, HEADS * DIM), 0)
    attended = jnp.where(row_at < len_ref[0], landed[0, 1].astype(F32), 0.0)
    gated[...] = (attended * gate[...].astype(F32)).astype(BF16)
    gate_grad[...] = (attended * outgrad[...].astype(F32)).astype(BF16)
    q_grad[...] = landed[0, 0]
    k_grad[...] = landed[1, 0]
    v_grad[...] = landed[1, 1]
    rab_grad[...] = rab_in[:HEADS, :BANDS]


def body(queries, keys, values, gates, lengths, rab_steps, out_grad):
    block = (2, 2, HALF, DIM)
    any_space = pl.BlockSpec(memory_space=pl.ANY)
    smem = pl.BlockSpec(memory_space=pltpu.SMEM)
    vmem = pl.BlockSpec(memory_space=pltpu.VMEM)
    dma = pltpu.SemaphoreType.DMA
    landed, rab_part = pl.pallas_call(
        kernel,
        out_shape=(
            jax.ShapeDtypeStruct((2, 2, ROWS, HEADS * DIM), BF16),
            jax.ShapeDtypeStruct((8, DIM), F32),
        ),
        in_specs=[any_space] * 5 + [smem] * 2,
        out_specs=(vmem, vmem),
        scratch_shapes=[
            pltpu.VMEM((2, 2, ROWS, HEADS * DIM), BF16),
            pltpu.VMEM((2, ROWS, HEADS * DIM), BF16),
            pltpu.VMEM((6,) + block, BF16),
            pltpu.VMEM((6,) + block, F32),
            pltpu.VMEM((4,) + block, BF16),
            pltpu.VMEM((5,) + block, BF16),
            pltpu.VMEM((2,) + block, BF16),
            pltpu.VMEM((2, 2, ROWS, HEADS * DIM), BF16),
            pltpu.SMEM((BANDS + 1,), F32),
            pltpu.VMEM((BANDS, 8, HALF), F32),
            pltpu.VMEM((BANDS, 8, HALF), F32),
            pltpu.VMEM((4, 8, DIM), F32),
            pltpu.VMEM((4, 8, 8, DIM), F32),
            dma((5,)),
            dma((3, 2)),
            dma((3, 2)),
            dma((5, 2)),
            dma((4, 2)),
            dma((4, 2)),
            dma((5, 2)),
            dma((3, 2)),
            dma((3, 2)),
            dma((4, 8)),
            dma((4, 8)),
        ],
        compiler_params=pltpu.CompilerParams(
            collective_id=0, has_side_effects=True, vmem_limit_bytes=60 * 2**20
        ),
        name="attend",
    )(queries[0], keys[0], values[0], gates[0], out_grad[0], lengths, rab_steps)
    shape = jax.ShapeDtypeStruct((ROWS, HEADS * DIM), BF16)
    outs = pl.pallas_call(
        closing,
        out_shape=(shape,) * 5 + (jax.ShapeDtypeStruct((HEADS, BANDS), F32),),
        in_specs=[vmem] * 4 + [smem],
        out_specs=(vmem,) * 6,
        name="closing",
    )(landed, rab_part, gates[0], out_grad[0], lengths)
    return tuple(out[None] for out in outs[:5]) + (outs[5],)


def solution(mesh):
    rows = P("dp", "seq", None)
    return jax.shard_map(
        body,
        mesh=mesh,
        in_specs=(rows, rows, rows, rows, P("dp"), P(), rows),
        out_specs=(rows, rows, rows, rows, rows, P()),
        check_vma=False,
    )
```

```python
import functools

import jax
import jax.numpy as jnp
from jax import lax
from jax.experimental import pallas as pl
from jax.experimental.pallas import tpu as pltpu
from jax.sharding import PartitionSpec as P

MESH = pl.DeviceIdType.MESH
BF16, F32 = jnp.bfloat16, jnp.float32
HEADS, DIM, BANDS = 4, 128, 16
ROWS, HALF = 128, 256
DEAD = -20000.0


def nt(a, b):
    return lax.dot_general(a, b, (((1,), (1,)), ((), ())), preferred_element_type=F32)


def nn(a, b):
    return jnp.dot(a, b, preferred_element_type=F32)


def tn(a, b):
    return lax.dot_general(a, b, (((0,), (0,)), ((), ())), preferred_element_type=F32)


def kernel(
    q_hbm, k_hbm, v_hbm, gate_hbm, og_hbm, len_ref, rab_ref,
    out_ref, rab_out,
    src, raw, obj, acc, snd, ret, stg, land, csm, low, tot,
    msg, got,
    l_sem, a_s, a_r, f_s, f_r, b_s, b_r, o_s, o_r, r_s, r_r,
):
    dp, sq = lax.axis_index("dp"), lax.axis_index("seq")
    y, xl = dp // 4, dp % 4
    z, xh, c = sq // 4, (sq // 2) % 2, sq % 2
    head = 2 * xh + c
    sign = 1 - 2 * c
    zp = c * 7 + sign * z
    prim, sec = 1 - c, c
    near, far = xh, 1 - xh

    def plane(rel):
        other_x = 1 - xh if rel & 2 else xh
        other_c = 1 - c if rel & 1 else c
        return other_x, other_c

    def at_plane(rel):
        other_x, other_c = plane(rel)
        return {"seq": z * 4 + other_x * 2 + other_c}

    def at_z(step):
        return {"seq": ((z + step * sign + 8) % 8) * 4 + xh * 2 + c}

    barrier = pltpu.get_barrier_semaphore()
    for rel in (1, 2, 3):
        pl.semaphore_signal(barrier, inc=1, device_id=at_plane(rel), device_id_type=MESH)
    for step in range(1, 8):
        pl.semaphore_signal(barrier, inc=1, device_id=at_z(step), device_id_type=MESH)
        pl.semaphore_signal(barrier, inc=1, device_id={"dp": ((y + step) % 8) * 4 + xl}, device_id_type=MESH)
    for step in range(1, 4):
        pl.semaphore_signal(barrier, inc=1, device_id={"dp": y * 4 + (xl + step) % 4}, device_id_type=MESH)

    loads = [
        pltpu.make_async_copy(gate_hbm, raw.at[0], l_sem.at[0]),
        pltpu.make_async_copy(og_hbm, raw.at[1], l_sem.at[1]),
        pltpu.make_async_copy(q_hbm, src.at[0, 0], l_sem.at[2]),
        pltpu.make_async_copy(k_hbm, src.at[1, 0], l_sem.at[3]),
        pltpu.make_async_copy(v_hbm, src.at[1, 1], l_sem.at[4]),
    ]
    for load in loads:
        load.start()
    csm[0] = jnp.float32(DEAD)
    level = jnp.float32(0.0)
    for band in range(BANDS):
        level = level + rab_ref[head, band]
        csm[band + 1] = level * 0.5
    for load in loads[:2]:
        load.wait()
    row_at = sq * ROWS + lax.broadcasted_iota(jnp.int32, (ROWS, HEADS * DIM), 0)
    dgrad = raw[0].astype(F32) * raw[1].astype(F32)
    src[0, 1] = jnp.where(row_at < len_ref[0], dgrad, 0.0).astype(BF16)
    for load in loads[2:]:
        load.wait()
    pl.semaphore_wait(barrier, 20)

    def head_cols(which):
        return pl.ds(pl.multiple_of(which * DIM, DIM), DIM)

    def own_rows(which):
        return pl.ds(pl.multiple_of(which * ROWS, ROWS), ROWS)

    def exchange(rel, which):
        other_x, other_c = plane(rel)
        return pltpu.make_async_remote_copy(
            src_ref=src.at[which, :, :, head_cols(2 * other_x + other_c)],
            dst_ref=obj.at[which, xh, :, own_rows(c), :],
            send_sem=a_s.at[rel - 1, which],
            recv_sem=a_r.at[rel - 1, which],
            device_id=at_plane(rel),
            device_id_type=MESH,
        )

    def arrival(rel, which):
        other_x, other_c = plane(rel)
        return pltpu.make_async_remote_copy(
            src_ref=src.at[which, :, :, head_cols(head)],
            dst_ref=obj.at[which, other_x, :, own_rows(other_c), :],
            send_sem=a_s.at[rel - 1, which],
            recv_sem=a_r.at[rel - 1, which],
            device_id=at_plane(rel),
            device_id_type=MESH,
        )

    def leading(core):
        up = jnp.where(z >= 6, 0, 1)
        down = jnp.where(z < 2, 1, 0)
        return jnp.where(core == 0, up, down)

    mine, theirs = leading(c), leading(1 - c)
    exchange(2, mine).start()
    exchange(3, theirs).start()
    exchange(1, theirs).start()
    exchange(2, 1 - mine).start()
    exchange(3, 1 - theirs).start()
    exchange(1, 1 - theirs).start()
    for which in (0, 1):
        for part in (0, 1):
            obj[which, xh, part, own_rows(c), :] = src[which, part, :, head_cols(head)]

    def move(source, hop, dist, half, kind):
        return pltpu.make_async_remote_copy(
            src_ref=obj.at[source, half],
            dst_ref=obj.at[1 + dist, half],
            send_sem=f_s.at[kind, half],
            recv_sem=f_r.at[dist - 1, half],
            device_id=at_z(hop),
            device_id_type=MESH,
        )

    late = jnp.where(zp < 7, prim, sec)

    def to_one(half):
        return move(late, 1, 1, half, 0)

    def to_two(half):
        return move(jnp.where(zp < 6, prim, sec), 2, 2, half, 1)

    def pass_three(half):
        return move(3, 1, 3, half, 2)

    def pass_four(half):
        return move(3, 2, 4, half, 3)

    def to_three(half):
        return move(sec, 3, 3, half, 4)

    gives_three = zp != 7
    gives_four = zp <= 3
    has_four = (zp >= 2) & (zp <= 5)
    jumps = (zp == 5) | (zp == 6)

    def sums_up(dist):
        return (zp >= 1) & (zp <= 4) if dist == 3 else zp != 7

    def pass_on(half):
        move(0, 2, 2, half, 1).wait_recv()

        @pl.when(gives_three)
        def _():
            pass_three(half).start()

        @pl.when(gives_four)
        def _():
            pass_four(half).start()

    def leave(half):
        to_two(half).start()

        @pl.when(zp != 6)
        def _():
            to_one(half).start()

    arrival(1, mine).wait_recv()
    leave(near)
    acc[...] = jnp.zeros_like(acc)
    low[...] = jnp.zeros_like(low)
    tot[...] = jnp.zeros_like(tot)
    arrival(2, mine).wait_recv()
    arrival(3, mine).wait_recv()
    leave(far)
    pass_on(near)
    pass_on(far)
    for rel in (1, 2, 3):
        arrival(rel, 1 - mine).wait_recv()

    @pl.when(zp == 6)
    def _():
        to_one(near).start()
        to_one(far).start()

    @pl.when(zp == 5)
    def _():
        to_three(near).start()
        to_three(far).start()

    row = lax.broadcasted_iota(jnp.int32, (HALF, HALF), 0)
    col = lax.broadcasted_iota(jnp.int32, (HALF, HALF), 1)
    lower = row >= col

    def fold(tile):
        return jnp.sum(tile.reshape(HALF // 8, 8, HALF), axis=0)

    def pair(q_slot, q_half, k_slot, k_half, gap):
        query, dgr = obj[q_slot, q_half, 0], obj[q_slot, q_half, 1]
        key, value = obj[k_slot, k_half, 0], obj[k_slot, k_half, 1]
        half_act = nt(query, key) * (0.5 * DIM**-0.5) + jnp.where(lower, csm[gap + 1], csm[gap])
        th = jnp.tanh(half_act)
        up = 1.0 + th
        weight = (half_act * up).astype(BF16)
        dpre = nt(dgr, value) * (up * (1.0 + half_act * (1.0 - th)))
        dhalf = dpre.astype(BF16)
        acc[q_slot, q_half, 1] += nn(weight, value)
        acc[q_slot, q_half, 0] += nn(dhalf, key)
        acc[k_slot, k_half, 1] += tn(weight, dgr)
        acc[k_slot, k_half, 0] += tn(dhalf, query)
        tot[gap] += fold(dpre)
        low[gap] += fold(jnp.where(lower, dpre, 0.0))

    def diagonal(index, unused):
        q_half, k_half = jnp.minimum(index, 1), index // 2
        pair(0, q_half, 1, k_half, q_half - k_half)
        return unused

    lax.fori_loop(0, 3, diagonal, 0)

    def chunk(index, unused):
        dist = index // 2 + 1
        half = jnp.where(index % 2 == 0, near, far)

        @pl.when(dist != 2)
        def _():
            move(0, 1, dist, half, 0).wait_recv()

        slot = 1 + dist
        direct = zp >= dist
        kind = jnp.where(direct, prim, sec)
        gap = 2 * jnp.where(direct, dist, 8 - dist)
        q_slot = jnp.where(kind == 0, slot, 0)
        k_slot = jnp.where(kind == 0, 1, slot)
        for other in (0, 1):
            q_half = jnp.where(kind == 0, half, other)
            k_half = jnp.where(kind == 0, other, half)
            pair(q_slot, q_half, k_slot, k_half, gap + q_half - k_half)
        return unused

    lax.fori_loop(0, jnp.where(has_four, 8, 6), chunk, 0)

    def give_back(dist, half):
        jumped = (zp == 0) if dist == 3 else False
        hop = 2 if dist == 2 else jnp.where(jumped, 3, 1)
        place = jnp.where(jumped, 4, dist - 1)
        return pltpu.make_async_remote_copy(
            src_ref=snd.at[dist - 1, half],
            dst_ref=ret.at[place, half],
            send_sem=b_s.at[dist - 1, half],
            recv_sem=b_r.at[place, half],
            device_id=at_z(-hop),
            device_id_type=MESH,
        )

    def take_back(slot, place, half):
        pltpu.make_async_remote_copy(
            src_ref=snd.at[0, half],
            dst_ref=ret.at[place, half],
            send_sem=b_s.at[0, half],
            recv_sem=b_r.at[place, half],
            device_id=at_z(-1),
            device_id_type=MESH,
        ).wait_recv()
        acc[slot, half] += ret[place, half].astype(F32)

    def send_back(dist, half):
        if dist in (2, 3):
            @pl.when(sums_up(dist))
            def _():
                take_back(1 + dist, dist, half)

        snd[dist - 1, half] = acc[1 + dist, half].astype(BF16)
        give_back(dist, half).start()

    rows_out = [None] * BANDS
    running = jnp.zeros((1, HALF), F32)
    for band in range(BANDS - 1, -1, -1):
        rows_out[band] = running + jnp.sum(low[band], axis=0, keepdims=True)
        running = running + jnp.sum(tot[band], axis=0, keepdims=True)
    per_band = jnp.sum(jnp.concatenate(rows_out, axis=0), axis=1, keepdims=True)
    lane = lax.broadcasted_iota(jnp.int32, (BANDS, DIM), 1)
    line = lax.broadcasted_iota(jnp.int32, (BANDS, DIM), 0)
    spread = jnp.sum(jnp.where(lane == line, per_band, 0.0), axis=0, keepdims=True)
    place = lax.broadcasted_iota(jnp.int32, (8, DIM), 0)
    share = jnp.where(place == head, spread * (0.5 / 64.0 / 4096.0), 0.0)

    def stage(phase):
        if phase == 0:
            return 8, z, lambda other: {"seq": other * 4 + head}
        if phase == 1:
            return 4, head, lambda other: {"seq": z * 4 + other}
        if phase == 2:
            return 4, xl, lambda other: {"dp": y * 4 + other}
        return 8, y, lambda other: {"dp": other * 4 + xl}

    def share_with(phase, step):
        count, here, place_of = stage(phase)
        other = (here + step) % count
        return pltpu.make_async_remote_copy(
            src_ref=msg.at[phase],
            dst_ref=got.at[phase, here],
            send_sem=r_s.at[phase, step],
            recv_sem=r_r.at[phase, here],
            device_id=place_of(other),
            device_id_type=MESH,
        )

    def shared_by(phase, step):
        count, here, place_of = stage(phase)
        other = (here + step) % count
        return pltpu.make_async_remote_copy(
            src_ref=msg.at[phase],
            dst_ref=got.at[phase, other],
            send_sem=r_s.at[phase, step],
            recv_sem=r_r.at[phase, other],
            device_id=place_of(other),
            device_id_type=MESH,
        )

    def send_share(phase, value):
        count, here, _ = stage(phase)
        msg[phase] = value
        for step in range(1, count):
            share_with(phase, step).start()
        got[phase, here] = value

    def sum_shares(phase):
        count, _, _ = stage(phase)
        for step in range(1, count):
            shared_by(phase, step).wait_recv()
        total = got[phase, 0]
        for other in range(1, count):
            total = total + got[phase, other]
        return total

    send_share(0, share)

    for half in (far, near):
        @pl.when(has_four)
        def _():
            send_back(4, half)

        send_back(1, half)

    def deliver(rel, which):
        other_x, other_c = plane(rel)
        return pltpu.make_async_remote_copy(
            src_ref=stg.at[which, other_x, :, own_rows(other_c), :],
            dst_ref=land.at[which, :, :, head_cols(head)],
            send_sem=o_s.at[rel - 1, which],
            recv_sem=o_r.at[rel - 1, which],
            device_id=at_plane(rel),
            device_id_type=MESH,
        )

    def delivered(rel, which):
        other_x, other_c = plane(rel)
        return pltpu.make_async_remote_copy(
            src_ref=stg.at[which, other_x, :, own_rows(other_c), :],
            dst_ref=land.at[which, :, :, head_cols(2 * other_x + other_c)],
            send_sem=o_s.at[rel - 1, which],
            recv_sem=o_r.at[rel - 1, which],
            device_id=at_plane(rel),
            device_id_type=MESH,
        )

    def finish(which, half, is_far):
        stg[which, half, 0] = (acc[which, half, 0] * (DIM**-0.5 * 0.5 / 64.0)).astype(BF16)
        stg[which, half, 1] = (acc[which, half, 1] * (1.0 / 64.0)).astype(BF16)
        if is_far:
            deliver(2, which).start()
            deliver(3, which).start()
        else:
            deliver(1, which).start()
            for part in (0, 1):
                land[which, part, :, head_cols(head)] = stg[which, half, part, own_rows(c), :]

    @pl.when(jnp.logical_not(jumps))
    def _():
        finish(1 - late, far, True)
        finish(1 - late, near, False)

    send_back(3, far)
    send_back(3, near)
    send_share(1, sum_shares(0))
    send_back(2, far)
    send_back(2, near)
    send_share(2, sum_shares(1))
    for half, is_far in ((far, True), (near, False)):
        take_back(late, 0, half)
        take_back(jnp.where(zp < 6, prim, sec), 1, half)

        @pl.when(zp == 5)
        def _():
            take_back(sec, 4, half)

        finish(late, half, is_far)

        @pl.when(jumps)
        def _():
            finish(1 - late, half, is_far)

    send_share(3, sum_shares(2))
    for which in (0, 1):
        for rel in (1, 2, 3):
            delivered(rel, which).wait_recv()
    rab_out[...] = sum_shares(3)
    out_ref[...] = land[...]
    for phase in range(4):
        for step in range(1, stage(phase)[0]):
            share_with(phase, step).wait_send()

    for which in (0, 1):
        for rel in (1, 2, 3):
            exchange(rel, which).wait_send()
            deliver(rel, which).wait_send()
    for half in (far, near):
        to_one(half).wait_send()
        to_two(half).wait_send()

        @pl.when(gives_three)
        def _():
            pass_three(half).wait_send()

        @pl.when(gives_four)
        def _():
            pass_four(half).wait_send()

        @pl.when(zp == 5)
        def _():
            to_three(half).wait_send()

        for dist in (1, 2, 3):
            give_back(dist, half).wait_send()

        @pl.when(has_four)
        def _():
            give_back(4, half).wait_send()


def closing(landed, rab_in, gate, outgrad, len_ref, gated, q_grad, k_grad, v_grad, gate_grad, rab_grad):
    row_at = lax.axis_index("seq") * ROWS + lax.broadcasted_iota(jnp.int32, (ROWS, HEADS * DIM), 0)
    attended = jnp.where(row_at < len_ref[0], landed[0, 1].astype(F32), 0.0)
    gated[...] = (attended * gate[...].astype(F32)).astype(BF16)
    gate_grad[...] = (attended * outgrad[...].astype(F32)).astype(BF16)
    q_grad[...] = landed[0, 0]
    k_grad[...] = landed[1, 0]
    v_grad[...] = landed[1, 1]
    rab_grad[...] = rab_in[:HEADS, :BANDS]


def body(queries, keys, values, gates, lengths, rab_steps, out_grad):
    block = (2, 2, HALF, DIM)
    any_space = pl.BlockSpec(memory_space=pl.ANY)
    smem = pl.BlockSpec(memory_space=pltpu.SMEM)
    vmem = pl.BlockSpec(memory_space=pltpu.VMEM)
    dma = pltpu.SemaphoreType.DMA
    landed, rab_part = pl.pallas_call(
        kernel,
        out_shape=(
            jax.ShapeDtypeStruct((2, 2, ROWS, HEADS * DIM), BF16),
            jax.ShapeDtypeStruct((8, DIM), F32),
        ),
        in_specs=[any_space] * 5 + [smem] * 2,
        out_specs=(vmem, vmem),
        scratch_shapes=[
            pltpu.VMEM((2, 2, ROWS, HEADS * DIM), BF16),
            pltpu.VMEM((2, ROWS, HEADS * DIM), BF16),
            pltpu.VMEM((6,) + block, BF16),
            pltpu.VMEM((6,) + block, F32),
            pltpu.VMEM((4,) + block, BF16),
            pltpu.VMEM((5,) + block, BF16),
            pltpu.VMEM((2,) + block, BF16),
            pltpu.VMEM((2, 2, ROWS, HEADS * DIM), BF16),
            pltpu.SMEM((BANDS + 1,), F32),
            pltpu.VMEM((BANDS, 8, HALF), F32),
            pltpu.VMEM((BANDS, 8, HALF), F32),
            pltpu.VMEM((4, 8, DIM), F32),
            pltpu.VMEM((4, 8, 8, DIM), F32),
            dma((5,)),
            dma((3, 2)),
            dma((3, 2)),
            dma((5, 2)),
            dma((4, 2)),
            dma((4, 2)),
            dma((5, 2)),
            dma((3, 2)),
            dma((3, 2)),
            dma((4, 8)),
            dma((4, 8)),
        ],
        compiler_params=pltpu.CompilerParams(
            collective_id=0, has_side_effects=True, vmem_limit_bytes=60 * 2**20
        ),
        name="attend",
    )(queries[0], keys[0], values[0], gates[0], out_grad[0], lengths, rab_steps)
    shape = jax.ShapeDtypeStruct((ROWS, HEADS * DIM), BF16)
    outs = pl.pallas_call(
        closing,
        out_shape=(shape,) * 5 + (jax.ShapeDtypeStruct((HEADS, BANDS), F32),),
        in_specs=[vmem] * 4 + [smem],
        out_specs=(vmem,) * 6,
        name="closing",
    )(landed, rab_part, gates[0], out_grad[0], lengths)
    return tuple(out[None] for out in outs[:5]) + (outs[5],)


def solution(mesh):
    rows = P("dp", "seq", None)
    return jax.shard_map(
        body,
        mesh=mesh,
        in_specs=(rows, rows, rows, rows, P("dp"), P(), rows),
        out_specs=(rows, rows, rows, rows, rows, P()),
        check_vma=False,
    )
```
